128 devices in a mesh: spatial: 32 (over x, y, core), chan: 4 (over z).
Axes of the slice: x: 4, y: 4, z: 4, core: 2. Of those that a mesh axis runs over, the one named last changes fastest.
Arguments:
- fields: bfloat16 [1, 256, 737280], P(None, 'chan', 'spatial'), may hold values from -6 to 6
- mixing_weight: bfloat16 [2, 256, 256], P(None, 'chan'), may hold values from -0.25 to 0.25
- degree_gain: bfloat16 [640, 256], P(None, 'chan'), may hold values from 0.25 to 4
- cotangent: bfloat16 [1, 256, 737280], P(None, 'chan', 'spatial'), may hold values from -6 to 6
- order_ids: int32 [256], replicated, may hold values from 0 to 639, as said below
Outputs:
- output_field: bfloat16 [1, 256, 737280], P(None, 'chan', 'spatial')
- field_grad: bfloat16 [1, 256, 737280], P(None, 'chan', 'spatial')
- weight_grad: float32 [2, 256, 256], P(None, 'chan')
- gain_grad: float32 [640, 256], P(None, 'chan')
The draws below stay inside these ranges and needn't reach their ends.
Inputs may be any that keep to these rules, and one draw needn't show every extreme that they name: `order_ids`: 256 distinct orders in ascending order; 0 and 639 are always among them.
All inputs are finite; a program needn't handle non-finite values.
Results may differ from the reference program's by a relative error of at most 0.022.
Values may be sent and summed in bfloat16 or wider, within the bound.
A program may use at most 128 MiB of HBM per device.

```python
import math
import jax
import jax.numpy as jnp
from jax import lax

NLON = 1440
C = 256
LMAX = 640
MEMBERS = 1
NLAT = 512
ORDERS = 256


def draw_order_ids(key, part):
    key = jax.random.fold_in(key, 7)
    inner = jax.random.permutation(key, LMAX - 2)[:ORDERS - 2] + 1
    chosen = jnp.concatenate([jnp.array([0, LMAX - 1], dtype=jnp.int32), inner.astype(jnp.int32)])
    return jnp.sort(chosen).astype(jnp.int32)


def levels(key, dims, split, smallest, high):
    level, own = 1.0, jax.random.fold_in(key, 6)
    for axis_at, parts in split:
        heights = jnp.exp(jax.random.uniform(jax.random.fold_in(own, axis_at), (parts,), jnp.float32, smallest / len(split), high / len(split)))
        level = level * jnp.repeat(heights, dims[axis_at] // parts).reshape([-1 if axis == axis_at else 1 for axis in range(len(dims))])
    return level


def scatter_about(stream_key, extent, spread, reach, split=(), kind=jnp.bfloat16):
    loudness = levels(stream_key, extent, split, -0.22, 0.18) if split else 1.0
    entries = jax.random.normal(stream_key, extent, jnp.float32) * spread * loudness
    return jnp.minimum(jnp.maximum(entries, -reach), reach).astype(kind)


def setup_inputs(seed: int = 0) -> dict:
    seeds = jax.random.split(jax.random.key(seed), 6)
    return {
        "fields": scatter_about(seeds[0], (MEMBERS, C, NLAT * NLON), 1.0, 6.0, ((1, 4), (2, 32))),
        "mixing_weight": scatter_about(seeds[1], (2, C, C), (2 * C) ** -0.5, 0.25, ((1, 4),)),
        "degree_gain": jnp.clip(jnp.exp(math.log(4.0) - 2.7725887 * jax.random.uniform(seeds[2], (LMAX, C), jnp.float32) ** levels(seeds[2], (LMAX, C), ((1, 4),), -0.2, 0.2)), 0.25, 4.0).astype(jnp.bfloat16),
        "cotangent": scatter_about(seeds[3], (MEMBERS, C, NLAT * NLON), 1.0, 6.0, ((1, 4), (2, 32))),
        "order_ids": draw_order_ids(jax.random.fold_in(seeds[5], 71), 0),
    }


def fourier_table(orders, lon_count, factor):
    longitude = jnp.arange(lon_count, dtype=jnp.int32)
    residue = longitude[:, None] * orders[None, :].astype(jnp.int32) % lon_count
    angles = residue.astype(jnp.float32) * (2.0 * math.pi / lon_count)
    result_table = jnp.stack([jnp.cos(angles), -jnp.sin(angles)], axis=2) * factor
    return result_table.astype(jnp.bfloat16)

def legendre_table(orders, degree_count, lat_count):
    degree = jnp.arange(degree_count, dtype=jnp.int32)
    latitude = jnp.arange(lat_count, dtype=jnp.int32)
    residue = (2 * degree[:, None] + 1) * (2 * latitude[None, :] + 1) % (8 * lat_count)
    base_angle = residue.astype(jnp.float32) * (math.pi / (4 * lat_count))
    angles = base_angle[None, :, :] + 0.37 * orders.astype(jnp.float32)[:, None, None]
    inside = degree[None, :, None] >= orders.astype(jnp.int32)[:, None, None]
    values = jnp.where(inside, jnp.cos(angles) * math.sqrt(2.0 / lat_count), 0.0)
    return values.astype(jnp.bfloat16)

def gelu_parts(values):
    normal_cdf = 0.5 * (1.0 + lax.erf(values * 0.7071067811865476))
    density = jnp.exp(-0.5 * values * values) * 0.3989422804014327
    return (values * normal_cdf, normal_cdf + values * density)

def big_matrix(weight):
    real_part = weight[0]
    imag_part = weight[1]
    upper_rows = jnp.concatenate([real_part, imag_part], axis=1)
    lower_rows = jnp.concatenate([-imag_part, real_part], axis=1)
    return jnp.concatenate([upper_rows, lower_rows], axis=0)

def split_matrix(matrix):
    rows_half = matrix.shape[0] // 2
    cols_half = matrix.shape[1] // 2
    real_part = matrix[:rows_half, :cols_half] + matrix[rows_half:, cols_half:]
    imag_part = matrix[:rows_half, cols_half:] - matrix[rows_half:, :cols_half]
    return jnp.stack([real_part, imag_part])

def legendre_apply(order_ids, data, formula):
    order_groups = order_ids.reshape(-1, 8)
    batched = data.reshape((order_groups.shape[0], 8, data.shape[1], -1))

    def one_group(group_args):
        orders, block_data = group_args
        result_table = legendre_table(orders, LMAX, NLAT).astype(jnp.float32)
        return jnp.einsum(formula, result_table, block_data.astype(jnp.float32))
    result = lax.map(one_group, (order_groups, batched))
    return result.reshape((ORDERS, -1, MEMBERS, 2, C))

def reference(fields, mixing_weight, degree_gain, cotangent, order_ids):
    forward_table = fourier_table(order_ids, NLON, 1.0 / math.sqrt(NLON)).astype(jnp.float32)
    inverse_table = fourier_table(order_ids, NLON, 1.0 / math.sqrt(ORDERS)).astype(jnp.float32)
    grid_in = fields.reshape(MEMBERS, C, NLAT, NLON).astype(jnp.float32)
    spectral_in = jnp.einsum('ecan,nmp->maepc', grid_in, forward_table).astype(jnp.bfloat16)
    coeffs = legendre_apply(order_ids, spectral_in, 'mlj,mjk->mlk').astype(jnp.bfloat16)
    matrix = big_matrix(mixing_weight)
    mixed_coeffs = jnp.dot(coeffs.reshape(-1, 2 * C), matrix, preferred_element_type=jnp.float32).reshape(coeffs.shape)
    gain_wide = degree_gain.astype(jnp.float32)[None, :, None, None, :]
    scaled = (gain_wide * mixed_coeffs).astype(jnp.bfloat16)
    grid_coeffs = legendre_apply(order_ids, scaled, 'mlj,mlk->mjk').astype(jnp.bfloat16)
    before = jnp.einsum('maepc,nmp->ecan', grid_coeffs.astype(jnp.float32), inverse_table)
    activated, derivative = gelu_parts(before)
    grid_cot = cotangent.reshape(MEMBERS, C, NLAT, NLON).astype(jnp.float32)
    grad_before = (grid_cot * derivative).astype(jnp.bfloat16)
    grad_grid = jnp.einsum('ecan,nmp->maepc', grad_before.astype(jnp.float32), inverse_table).astype(jnp.bfloat16)
    grad_scaled = legendre_apply(order_ids, grad_grid, 'mlj,mjk->mlk')
    gain_grad = lax.optimization_barrier(jnp.sum(grad_scaled * mixed_coeffs, axis=(0, 2, 3))) * (1.0 / math.sqrt(ORDERS))
    grad_mixed = (gain_wide * grad_scaled).astype(jnp.bfloat16)
    flat_grad = grad_mixed.reshape(-1, 2 * C)
    grad_inputs = jnp.dot(flat_grad, matrix.T, preferred_element_type=jnp.float32).astype(jnp.bfloat16).reshape(coeffs.shape)
    weight_grad = split_matrix(jnp.dot(coeffs.reshape(-1, 2 * C).T, flat_grad, preferred_element_type=jnp.float32))
    weight_grad = weight_grad * (1.0 / math.sqrt(ORDERS * LMAX))
    grad_spectral = legendre_apply(order_ids, grad_inputs, 'mlj,mlk->mjk').astype(jnp.bfloat16)
    field_grad = jnp.einsum('maepc,nmp->ecan', grad_spectral.astype(jnp.float32), forward_table).astype(jnp.bfloat16)
    output_field = activated.astype(jnp.bfloat16).reshape(MEMBERS, C, NLAT * NLON)
    return (output_field, field_grad.reshape(MEMBERS, C, NLAT * NLON), weight_grad, gain_grad)
```

```python
import functools
import math

import jax
import jax.numpy as jnp
from jax import lax
from jax.experimental import pallas as pl
from jax.experimental.pallas import tpu as pltpu
from jax.sharding import PartitionSpec as P

MESH = pl.DeviceIdType.MESH
BF = jnp.bfloat16
F32 = jnp.float32

NLON = 1440
NLAT = 512
LMAX = 640
ORD = 256
NS = 32
NZ = 4
ND = NS * NZ
CD = 64
GROUP = 4 * NLON
WIN = 1536
STARTS = tuple((NLON * r) // 128 * 128 for r in range(4))
RED = 576
RCH = 32
NCH = RED // RCH


def sincos(angle):
    h = angle * 0.5
    y = h * h
    s = y * (-1.0 / 39916800.0) + 1.0 / 362880.0
    s = s * y - 1.0 / 5040.0
    s = s * y + 1.0 / 120.0
    s = s * y - 1.0 / 6.0
    s = (s * y + 1.0) * h
    c = y * (1.0 / 479001600.0) - 1.0 / 3628800.0
    c = c * y + 1.0 / 40320.0
    c = c * y - 1.0 / 720.0
    c = c * y + 1.0 / 24.0
    c = c * y - 0.5
    c = c * y + 1.0
    return 2.0 * s * c, 1.0 - 2.0 * s * s


def turn(steps, period):
    rest = steps - period * jnp.floor(steps * (1.0 / period) + 0.5)
    return sincos(rest * (2.0 * math.pi / period))


def iota(shape, dim):
    return lax.broadcasted_iota(jnp.int32, shape, dim)


def gelu_parts(v):
    cdf = 0.5 * (1.0 + lax.erf(v * 0.7071067811865476))
    density = jnp.exp(-0.5 * v * v) * 0.3989422804014327
    return v * cdf, cdf + v * density


def swap_halves(a, b):
    low = iota(a.shape, 1) < 64
    return (
        jnp.where(low, a, pltpu.roll(b, 64, 1)),
        jnp.where(low, pltpu.roll(a, 64, 1), b),
    )


def dot_nn(a, b):
    return lax.dot_general(a, b, (((1,), (0,)), ((), ())), preferred_element_type=F32)


def dot_nt(a, b):
    return lax.dot_general(a, b, (((1,), (1,)), ((), ())), preferred_element_type=F32)


def dot_tn(a, b):
    return lax.dot_general(a, b, (((0,), (0,)), ((), ())), preferred_element_type=F32)


def kernel(
    x_hbm, w_ref, gain_ref, cot_hbm, ords_ref, ords_smem,
    out_hbm, fgrad_hbm, wgrad_ref, ggrad_ref,
    x_v, cot_v, out_v, tab, trig, leg, legt, scr,
    snd, rcv, wsend, wrecv, gsend, grecv, mat,
    acc, mixed, coeffs, spec, red, redin, mine, fin,
    in_sem, out_sem, ssem, rsem, wsem, wrsem,
):
    s = lax.axis_index("spatial")
    z = lax.axis_index("chan")
    me = s * NZ + z
    barrier = pltpu.get_barrier_semaphore()

    def greet(i, carry):
        t = (me + i * 37) % ND
        pl.semaphore_signal(barrier, inc=1, device_id=(t // NZ, t % NZ), device_id_type=MESH)
        return carry

    lax.fori_loop(1, ND, greet, 0)
    x_in = pltpu.make_async_copy(x_hbm, x_v, in_sem.at[0])
    x_in.start()
    cot_in = pltpu.make_async_copy(cot_hbm, cot_v, in_sem.at[1])
    cot_in.start()

    row = jnp.broadcast_to(ords_ref[...].astype(F32), (ORD, ORD))
    eye = iota((ORD, ORD), 0) == iota((ORD, ORD), 1)
    order_col = jnp.sum(jnp.where(eye, row, 0.0), axis=1, keepdims=True)
    lane = iota((ORD, 384), 1)
    step = jnp.where(lane < 256, lane - 128, (lane - 256) * 128).astype(F32)
    sin_all, cos_all = turn(order_col * step, float(NLON))
    trig[0] = sin_all
    trig[1] = cos_all

    def fourier_rows(i, carry):
        rows = pl.ds(pl.multiple_of(i * 64, 64), 64)
        sin_row = trig[0, rows, :]
        cos_row = trig[1, rows, :]
        at = iota((64, 128), 1)
        shifted = []
        for r in range(4):
            lo = 128 - 32 * r
            shifted.append((sin_row[:, lo : lo + 128], cos_row[:, lo : lo + 128]))
        for q in range(12):
            sa = jnp.broadcast_to(sin_row[:, 256 + q : 257 + q], (64, 128))
            ca = jnp.broadcast_to(cos_row[:, 256 + q : 257 + q], (64, 128))
            for r in range(4):
                sb, cb = shifted[r]
                even = ca * cb - sa * sb
                odd = -(sa * cb + ca * sb)
                if q == 0 and r > 0:
                    even = jnp.where(at < 32 * r, 0.0, even)
                    odd = jnp.where(at < 32 * r, 0.0, odd)
                if q == 11 and r < 3:
                    even = jnp.where(at >= 32 * r + 32, 0.0, even)
                    odd = jnp.where(at >= 32 * r + 32, 0.0, odd)
                tab[r, 0, rows, q * 128 : q * 128 + 128] = even.astype(BF)
                tab[r, 1, rows, q * 128 : q * 128 + 128] = odd.astype(BF)
        return carry

    lax.fori_loop(0, ORD // 64, fourier_rows, 0)

    def start_all(phase, half, to_spectral):
        k = phase * 2 + half

        def go(i, carry):
            t = (me + i * 37) % ND
            ts, tz = t // NZ, t % NZ
            if to_spectral:
                src, dst = snd.at[k, t], rcv.at[k, z * NS + s]
            else:
                src, dst = snd.at[k, tz * NS + ts], rcv.at[k, me]
            pltpu.make_async_remote_copy(
                src_ref=src, dst_ref=dst, send_sem=ssem.at[k], recv_sem=rsem.at[k],
                device_id=(ts, tz), device_id_type=MESH,
            ).start()
            return carry

        lax.fori_loop(1, ND, go, 0)
        if to_spectral:
            pltpu.make_async_copy(snd.at[k, me], rcv.at[k, z * NS + s], rsem.at[k]).start()
        else:
            pltpu.make_async_copy(snd.at[k, z * NS + s], rcv.at[k, me], rsem.at[k]).start()

    def wait_all(phase, half):
        k = phase * 2 + half
        pltpu.make_async_copy(rcv.at[k], rcv.at[k], rsem.at[k]).wait()

    def window(ref, r):
        return jnp.concatenate(
            [ref[:, g * GROUP + STARTS[r] : g * GROUP + STARTS[r] + WIN] for g in range(4)], axis=0
        )

    def table(r):
        return tab[r].reshape(2 * ORD, WIN)

    def fourier_tiles(rr, data, r, factor):
        prod = dot_nt(table(r), data) * factor
        for pair in range(2):
            lanes = slice(pair * 128, pair * 128 + 128)
            tiles = swap_halves(prod[:ORD, lanes], prod[ORD:, lanes])
            for i in range(2):
                scr[pl.ds((pair * 2 + i) * 2 + rr, ORD, stride=8), :] = tiles[i]

    def pack_send(phase, half):
        snd[phase * 2 + half] = scr[...].reshape(ND, 16, 128).astype(BF)

    def forward_half(half):
        for rr in range(2):
            r = half * 2 + rr
            fourier_tiles(rr, window(x_v, r), r, 1.0 / math.sqrt(NLON))
        pack_send(0, half)

    x_in.wait()
    forward_half(0)
    pl.semaphore_wait(barrier, ND - 1)
    start_all(0, 0, True)
    forward_half(1)
    start_all(0, 1, True)

    wsend[...] = w_ref[...].reshape(2 * CD, 256)
    gain_half = gain_ref[...].astype(F32)
    gsend[...] = jnp.concatenate([gain_half, gain_half], axis=1).astype(BF)
    for dz in range(1, NZ):
        tz = (z + dz) % NZ
        pltpu.make_async_remote_copy(
            src_ref=wsend, dst_ref=wrecv.at[z], send_sem=wsem.at[0], recv_sem=wrsem.at[0],
            device_id=(s, tz), device_id_type=MESH,
        ).start()
        pltpu.make_async_remote_copy(
            src_ref=gsend, dst_ref=grecv.at[z], send_sem=wsem.at[1], recv_sem=wrsem.at[1],
            device_id=(s, tz), device_id_type=MESH,
        ).start()
    pltpu.make_async_copy(wsend, wrecv.at[z], wrsem.at[0]).start()
    pltpu.make_async_copy(gsend, grecv.at[z], wrsem.at[1]).start()

    order_here = [ords_smem[2 * me + i].astype(F32) for i in range(2)]
    phase_sc = []
    for i in range(2):
        phi = jnp.full((16, 128), 1.0, F32) * (order_here[i] * 0.37)
        turns = jnp.floor(phi * (1.0 / (2.0 * math.pi)) + 0.5)
        phi = (phi - turns * 6.28125) - turns * (2.0 * math.pi - 6.28125)
        phase_sc.append(sincos(phi))

    def lat_of(at):
        place = at % 256
        return (place // 8) * 16 + ((place % 8) // 2) * 4 + (at // 256) * 2 + at % 2

    def with_phase(i, sn, cs):
        sp, cp = phase_sc[i]
        sp, cp = sp[:, :1], cp[:, :1]
        return sn * cp + cs * sp, cs * cp - sn * sp

    lat_odd = (2 * lat_of(iota((16, NLAT), 1)) + 1).astype(F32)
    base_s, base_c = turn((2 * iota((16, NLAT), 0) + 1).astype(F32) * lat_odd, 4096.0)
    base = [with_phase(i, base_s, base_c) for i in range(2)]

    def leg_rows(q, carry):
        first = q * 16
        sa, ca = turn((2 * first).astype(F32) * lat_odd[:8], 4096.0)
        sa, ca = jnp.concatenate([sa, sa], axis=0), jnp.concatenate([ca, ca], axis=0)
        degree = (first + iota((16, NLAT), 0)).astype(F32)
        for i in range(2):
            sb, cb = base[i]
            value = jnp.where(degree >= order_here[i], ca * cb - sa * sb, 0.0)
            leg[i, pl.ds(pl.multiple_of(first, 16), 16), :] = value.astype(BF)
        return carry

    lax.fori_loop(0, LMAX // 16, leg_rows, 0)

    deg_odd = (2 * iota((16, LMAX), 1) + 1).astype(F32)
    live = [iota((16, LMAX), 1).astype(F32) >= order_here[i] for i in range(2)]
    for half in range(2):
        r16 = iota((16, LMAX), 0)
        low = (r16 // 8) * 16 + ((r16 % 8) // 2) * 4 + 2 * half + r16 % 2
        bs, bc = turn((2 * low + 1).astype(F32) * deg_odd, 4096.0)
        tbase = [with_phase(i, bs, bc) for i in range(2)]

        def legt_rows(q, carry):
            sa, ca = turn((64 * q).astype(F32) * deg_odd[:8], 4096.0)
            sa, ca = jnp.concatenate([sa, sa], axis=0), jnp.concatenate([ca, ca], axis=0)
            for i in range(2):
                sb, cb = tbase[i]
                value = jnp.where(live[i], ca * cb - sa * sb, 0.0)
                legt[i, pl.ds(pl.multiple_of(half * 256 + q * 16, 16), 16), :] = value.astype(BF)
            return carry

        lax.fori_loop(0, 16, legt_rows, 0)

    def spectral_half(phase, half, finish):
        wait_all(phase, half)
        k = phase * 2 + half
        tiles = [rcv[k, zz * NS : zz * NS + NS].astype(F32) for zz in range(NZ)]
        for i in range(2):
            data = jnp.concatenate(
                [t[:, i * 8 : i * 8 + 8, :].reshape(256, 128) for t in tiles], axis=1
            ).astype(BF)
            prod = dot_nn(leg[i, :, half * 256 : half * 256 + 256], data)
            if half == 0:
                acc[i] = prod
            else:
                finish(i, (acc[i] + prod) * 0.0625)

    def grid_half(phase, half):
        k = phase * 2 + half
        parts = [
            dot_nn(legt[i, half * 256 : half * 256 + 256, :], spec[i]) * 0.0625 for i in range(2)
        ]
        for zz in range(NZ):
            lanes = slice(zz * 128, zz * 128 + 128)
            both = jnp.concatenate([p[:, lanes].reshape(NS, 8, 128) for p in parts], axis=1)
            snd[k, zz * NS : zz * NS + NS] = both.astype(BF)

    def keep_coeffs(i, value):
        coeffs[i] = value.astype(BF)

    spectral_half(0, 0, keep_coeffs)
    spectral_half(0, 1, keep_coeffs)

    pltpu.make_async_copy(wrecv, wrecv, wrsem.at[0]).wait()
    pltpu.make_async_copy(grecv, grecv, wrsem.at[1]).wait()
    for zz in range(NZ):
        w_real = wrecv[zz, :CD].astype(F32)
        w_imag = wrecv[zz, CD:].astype(F32)
        for u in range(2):
            a = w_real[:, u * 128 : u * 128 + 128]
            b = w_imag[:, u * 128 : u * 128 + 128]
            top = swap_halves(a, b)
            low = swap_halves(-b, a)
            for i in range(2):
                lanes = slice((2 * u + i) * 128, (2 * u + i) * 128 + 128)
                mat[zz * 128 : zz * 128 + CD, lanes] = top[i].astype(BF)
                mat[zz * 128 + CD : zz * 128 + 128, lanes] = low[i].astype(BF)

    def gains():
        return jnp.concatenate([grecv[zz] for zz in range(NZ)], axis=1).astype(F32)

    for i in range(2):
        prod = dot_nn(coeffs[i], mat[...])
        mixed[i] = prod
        spec[i] = (gains() * prod).astype(BF)

    grid_half(1, 0)
    start_all(1, 0, False)
    grid_half(1, 1)
    start_all(1, 1, False)

    def order_rows(phase, half, rr):
        tiles = [scr[pl.ds(g * 2 + rr, ORD, stride=8), :] for g in range(4)]
        pairs = [swap_halves(tiles[0], tiles[1]), swap_halves(tiles[2], tiles[3])]
        return jnp.concatenate(
            [jnp.concatenate([pairs[0][p], pairs[1][p]], axis=1) for p in range(2)], axis=0
        ).astype(BF)

    def put_window(ref, r, value):
        for g in range(4):
            part = value[g * CD : g * CD + CD]
            lo = g * GROUP + STARTS[r]
            if r > 0:
                first = ref[:, lo : lo + 128].astype(F32) + part[:, :128]
                ref[:, lo : lo + 128] = first.astype(BF)
                ref[:, lo + 128 : lo + WIN] = part[:, 128:].astype(BF)
            else:
                ref[:, lo : lo + WIN] = part.astype(BF)

    cot_in.wait()
    for half in range(2):
        wait_all(1, half)
        scr[...] = rcv[2 + half].astype(F32).reshape(ND * 16, 128)
        rows = [order_rows(1, half, rr) for rr in range(2)]
        for rr in range(2):
            r = half * 2 + rr
            before = dot_tn(rows[rr], table(r)) * 0.0625
            value, slope = gelu_parts(before)
            put_window(out_v, r, value)
            grad = (window(cot_v, r).astype(F32) * slope).astype(BF)
            fourier_tiles(rr, grad, r, 0.0625)
        pack_send(2, half)
        start_all(2, half, True)
    out_copy = pltpu.make_async_copy(out_v, out_hbm, out_sem.at[0])
    out_copy.start()

    def keep_grads(i, value):
        grad_here = value * mixed[i]
        if i == 0:
            acc[0] = grad_here
        else:
            acc[0] = acc[0] + grad_here
        spec[i] = (gains() * value).astype(BF)

    spectral_half(2, 0, keep_grads)
    spectral_half(2, 1, keep_grads)

    gmix = [spec[i] for i in range(2)]
    wpart = dot_tn(coeffs[0], gmix[0]) + dot_tn(coeffs[1], gmix[1])
    for i in range(2):
        spec[i] = dot_nt(spec[i], mat[...]).astype(BF)
    grid_half(3, 0)
    start_all(3, 0, False)
    grid_half(3, 1)
    start_all(3, 1, False)

    sign = jnp.where(iota((CD, 128), 1) < 64, 1.0, -1.0)
    for zz in range(NZ):
        for zo in range(NZ):
            lanes = slice(zo * 128, zo * 128 + 128)
            up = wpart[zz * 128 : zz * 128 + CD, lanes]
            down = wpart[zz * 128 + CD : zz * 128 + 128, lanes]
            sums = up + pltpu.roll(down, 64, 1) * sign
            for part in range(2):
                red[zz, zo * 2 + part] = sums[part * RCH : part * RCH + RCH].astype(BF)
        both = acc[0, :, zz * 128 : zz * 128 + 128]
        both = both + pltpu.roll(both, 64, 1)
        half_low = iota((320, 128), 1) < 64
        fold = jnp.where(half_low, both[:320], both[320:]).astype(BF)
        red[zz, 8:NCH] = fold.reshape(NCH - 8, RCH, 128)

    def reduce_go(i, carry):
        c, tz = i // NZ, i % NZ

        @pl.when(c * NZ + tz != me)
        def _():
            pltpu.make_async_remote_copy(
                src_ref=red.at[tz, c], dst_ref=redin.at[me], send_sem=wsem.at[2], recv_sem=wrsem.at[2],
                device_id=(c, tz), device_id_type=MESH,
            ).start()

        @pl.when(c * NZ + tz == me)
        def _():
            pltpu.make_async_copy(red.at[tz, c], redin.at[me], wrsem.at[2]).start()

        return carry

    lax.fori_loop(0, NCH * NZ, reduce_go, 0)

    for half in range(2):
        wait_all(3, half)
        scr[...] = rcv[6 + half].astype(F32).reshape(ND * 16, 128)
        rows = [order_rows(3, half, rr) for rr in range(2)]
        for rr in range(2):
            r = half * 2 + rr
            value = dot_tn(rows[rr], table(r)) * (1.0 / math.sqrt(NLON))
            put_window(x_v, r, value)
    fgrad_copy = pltpu.make_async_copy(x_v, fgrad_hbm, out_sem.at[1])
    fgrad_copy.start()

    @pl.when(s < NCH)
    def _():
        pltpu.make_async_copy(redin, redin, wrsem.at[2]).wait()
        mine[...] = jnp.sum(redin[...].astype(F32), axis=0)
        for ds in range(1, NS):
            pltpu.make_async_remote_copy(
                src_ref=mine, dst_ref=fin.at[s], send_sem=wsem.at[3], recv_sem=wrsem.at[3],
                device_id=((s + ds) % NS, z), device_id_type=MESH,
            ).start()
        pltpu.make_async_copy(mine, fin.at[s], wrsem.at[3]).start()
        for ds in range(1, NS):
            pltpu.make_async_copy(mine, mine, wsem.at[3]).wait()

    pltpu.make_async_copy(fin, fin, wrsem.at[3]).wait()
    wscale = 1.0 / math.sqrt(ORD * LMAX)
    for u in range(2):
        for part in range(2):
            first = fin[u * 4 + part]
            second = fin[u * 4 + 2 + part]
            pair = swap_halves(first, second)
            for p in range(2):
                wgrad_ref[p, part * RCH : part * RCH + RCH, u * 128 : u * 128 + 128] = pair[p] * wscale
    fold_all = fin[8:NCH].reshape(320, 128) * (1.0 / math.sqrt(ORD))
    ggrad_ref[:320] = fold_all[:, :64]
    ggrad_ref[320:] = fold_all[:, 64:]

    for k in range(8):
        pltpu.make_async_copy(snd.at[k, pl.ds(0, ND - 1)], snd.at[k, pl.ds(0, ND - 1)], ssem.at[k]).wait()
    for _ in range(NZ - 1):
        pltpu.make_async_copy(wsend, wsend, wsem.at[0]).wait()
        pltpu.make_async_copy(gsend, gsend, wsem.at[1]).wait()

    @pl.when(s < NCH)
    def _():
        pltpu.make_async_copy(redin.at[pl.ds(0, NCH * NZ - 1)], redin.at[pl.ds(0, NCH * NZ - 1)], wsem.at[2]).wait()

    @pl.when(s >= NCH)
    def _():
        pltpu.make_async_copy(redin.at[pl.ds(0, NCH * NZ)], redin.at[pl.ds(0, NCH * NZ)], wsem.at[2]).wait()

    out_copy.wait()
    fgrad_copy.wait()


def body(fields, mixing_weight, degree_gain, cotangent, order_ids):
    cells = fields.shape[2]
    vmem = pl.BlockSpec(memory_space=pltpu.VMEM)
    anyw = pl.BlockSpec(memory_space=pl.ANY)
    smem = pl.BlockSpec(memory_space=pltpu.SMEM)
    out, fgrad, wgrad, ggrad = pl.pallas_call(
        kernel,
        out_shape=(
            jax.ShapeDtypeStruct((CD, cells), BF),
            jax.ShapeDtypeStruct((CD, cells), BF),
            jax.ShapeDtypeStruct((2, CD, 256), F32),
            jax.ShapeDtypeStruct((LMAX, CD), F32),
        ),
        in_specs=[anyw, vmem, vmem, anyw, vmem, smem],
        out_specs=(anyw, anyw, vmem, vmem),
        scratch_shapes=[
            pltpu.VMEM((CD, cells), BF),
            pltpu.VMEM((CD, cells), BF),
            pltpu.VMEM((CD, cells), BF),
            pltpu.VMEM((4, 2, ORD, WIN), BF),
            pltpu.VMEM((2, ORD, 384), F32),
            pltpu.VMEM((2, LMAX, NLAT), BF),
            pltpu.VMEM((2, NLAT, LMAX), BF),
            pltpu.VMEM((ND * 16, 128), F32),
            pltpu.VMEM((8, ND, 16, 128), BF),
            pltpu.VMEM((8, ND, 16, 128), BF),
            pltpu.VMEM((2 * CD, 256), BF),
            pltpu.VMEM((NZ, 2 * CD, 256), BF),
            pltpu.VMEM((LMAX, 128), BF),
            pltpu.VMEM((NZ, LMAX, 128), BF),
            pltpu.VMEM((512, 512), BF),
            pltpu.VMEM((2, LMAX, 512), F32),
            pltpu.VMEM((2, LMAX, 512), F32),
            pltpu.VMEM((2, LMAX, 512), BF),
            pltpu.VMEM((2, LMAX, 512), BF),
            pltpu.VMEM((NZ, NCH, RCH, 128), BF),
            pltpu.VMEM((ND, RCH, 128), BF),
            pltpu.VMEM((RCH, 128), F32),
            pltpu.VMEM((NCH, RCH, 128), F32),
            pltpu.SemaphoreType.DMA((2,)),
            pltpu.SemaphoreType.DMA((2,)),
            pltpu.SemaphoreType.DMA((8,)),
            pltpu.SemaphoreType.DMA((8,)),
            pltpu.SemaphoreType.DMA((4,)),
            pltpu.SemaphoreType.DMA((4,)),
        ],
        compiler_params=pltpu.CompilerParams(
            collective_id=0, has_side_effects=True, vmem_limit_bytes=60 << 20
        ),
    )(
        fields.reshape(CD, cells), mixing_weight, degree_gain, cotangent.reshape(CD, cells),
        order_ids.reshape(1, ORD), order_ids,
    )
    return out.reshape(1, CD, cells), fgrad.reshape(1, CD, cells), wgrad, ggrad


def solution(mesh):
    return jax.shard_map(
        body,
        mesh=mesh,
        in_specs=(
            P(None, "chan", "spatial"),
            P(None, "chan", None),
            P(None, "chan"),
            P(None, "chan", "spatial"),
            P(),
        ),
        out_specs=(
            P(None, "chan", "spatial"),
            P(None, "chan", "spatial"),
            P(None, "chan", None),
            P(None, "chan"),
        ),
        check_vma=False,
    )
```

```python
import math

import jax
import jax.numpy as jnp
from jax import lax
from jax.experimental import pallas as pl
from jax.experimental.pallas import tpu as pltpu
from jax.sharding import PartitionSpec as P

MESH = pl.DeviceIdType.MESH
BF = jnp.bfloat16
F32 = jnp.float32

NLON = 1440
NLAT = 512
LMAX = 640
ORD = 256
NS = 32
NZ = 4
ND = NS * NZ
NXY = NS // 2
CD = 64
LD = 16
GROUP = 4 * NLON
WIN = 1536
STARTS = tuple((NLON * r) // 128 * 128 for r in range(4))
WROWS = 128
GROWS = 160
WCH = 16
GCH = 32
NG = 320 // GCH


def sincos(angle):
    h = angle * 0.5
    y = h * h
    s = y * (-1.0 / 39916800.0) + 1.0 / 362880.0
    s = s * y - 1.0 / 5040.0
    s = s * y + 1.0 / 120.0
    s = s * y - 1.0 / 6.0
    s = (s * y + 1.0) * h
    c = y * (1.0 / 479001600.0) - 1.0 / 3628800.0
    c = c * y + 1.0 / 40320.0
    c = c * y - 1.0 / 720.0
    c = c * y + 1.0 / 24.0
    c = c * y - 0.5
    c = c * y + 1.0
    return 2.0 * s * c, 1.0 - 2.0 * s * s


def turn(steps, period):
    rest = steps - period * jnp.floor(steps * (1.0 / period) + 0.5)
    return sincos(rest * (2.0 * math.pi / period))


def iota(shape, dim):
    return lax.broadcasted_iota(jnp.int32, shape, dim)


def gelu_parts(v):
    cdf = 0.5 * (1.0 + lax.erf(v * 0.7071067811865476))
    density = jnp.exp(-0.5 * v * v) * 0.3989422804014327
    return v * cdf, cdf + v * density


def low_half(shape):
    return iota(shape, 1) < 64


def swap_halves(a, b):
    low = low_half(a.shape)
    return (
        jnp.where(low, a, pltpu.roll(b, 64, 1)),
        jnp.where(low, pltpu.roll(a, 64, 1), b),
    )


def dot_nn(a, b):
    return lax.dot_general(a, b, (((1,), (0,)), ((), ())), preferred_element_type=F32)


def dot_nt(a, b):
    return lax.dot_general(a, b, (((1,), (1,)), ((), ())), preferred_element_type=F32)


def dot_tn(a, b):
    return lax.dot_general(a, b, (((0,), (0,)), ((), ())), preferred_element_type=F32)


def kernel(
    x_hbm, w_ref, gain_ref, cot_hbm, ords_ref, ords_smem,
    out_v, x_v, wgrad_ref, ggrad_ref,
    cot_v, tab, trig, leg, legt, scr,
    snd, rcv, gfold, wg, mat, gains,
    gsum, mixed, coeffs, spec, redw, redg, pairw, pairg, inw, ing, minew, mineg, finw, fing,
    in_sem, ssem, rsem, wsem, wrsem, dsem, drsem,
):
    s = lax.axis_index("spatial")
    z = lax.axis_index("chan")
    me = s * NZ + z
    core = s % 2
    xy = s // 2
    sibling = s + 1 - 2 * core
    barrier = pltpu.get_barrier_semaphore()

    def greet(i, carry):
        t = (me + i * 37) % ND
        pl.semaphore_signal(barrier, inc=1, device_id=(t // NZ, t % NZ), device_id_type=MESH)
        return carry

    lax.fori_loop(1, ND, greet, 0)
    x_in = pltpu.make_async_copy(x_hbm, x_v, in_sem.at[0])
    x_in.start()
    cot_in = pltpu.make_async_copy(cot_hbm, cot_v, in_sem.at[1])

    def fourier_table(i):
        row = jnp.broadcast_to(ords_ref[...].astype(F32), (ND, ORD))
        picked = iota((ND, ORD), 1) == 2 * iota((ND, ORD), 0) + i
        order_col = jnp.sum(jnp.where(picked, row, 0.0), axis=1, keepdims=True)
        lane = iota((ND, 384), 1)
        step = jnp.where(lane < 256, lane - 128, (lane - 256) * 128).astype(F32)
        sin_all, cos_all = turn(order_col * step, float(NLON))
        trig[0] = sin_all
        trig[1] = cos_all

        def some_rows(b, carry):
            rows = pl.ds(pl.multiple_of(b * 64, 64), 64)
            sin_row = trig[0, rows, :]
            cos_row = trig[1, rows, :]
            at = iota((64, 128), 1)
            shifted = []
            for r in range(4):
                lo = 128 - 32 * r
                shifted.append((sin_row[:, lo : lo + 128], cos_row[:, lo : lo + 128]))
            for q in range(12):
                sa = jnp.broadcast_to(sin_row[:, 256 + q : 257 + q], (64, 128))
                ca = jnp.broadcast_to(cos_row[:, 256 + q : 257 + q], (64, 128))
                for r in range(4):
                    sb, cb = shifted[r]
                    even = ca * cb - sa * sb
                    odd = -(sa * cb + ca * sb)
                    if q == 0 and r > 0:
                        even = jnp.where(at < 32 * r, 0.0, even)
                        odd = jnp.where(at < 32 * r, 0.0, odd)
                    if q == 11 and r < 3:
                        even = jnp.where(at >= 32 * r + 32, 0.0, even)
                        odd = jnp.where(at >= 32 * r + 32, 0.0, odd)
                    tab[r, i, 0, rows, q * 128 : q * 128 + 128] = even.astype(BF)
                    tab[r, i, 1, rows, q * 128 : q * 128 + 128] = odd.astype(BF)
            return carry

        lax.fori_loop(0, ND // 64, some_rows, 0)

    def start_all(phase, i, to_spectral, beside=None, count=0):
        k = phase * 2 + i

        def go(n, carry):
            t = (me + n * 37) % ND
            ts, tz = t // NZ, t % NZ
            if to_spectral:
                src, dst = snd.at[k, t], rcv.at[k, z * NS + s]
            else:
                src, dst = snd.at[k, tz * NS + ts], rcv.at[k, me]
            pltpu.make_async_remote_copy(
                src_ref=src, dst_ref=dst, send_sem=ssem.at[k], recv_sem=rsem.at[k],
                device_id=(ts, tz), device_id_type=MESH,
            ).start()
            return carry

        def go_both(n, carry):
            beside(n - 1)
            return go(n, carry)

        if count:
            lax.fori_loop(1, 1 + count, go_both, 0)
        lax.fori_loop(1 + count, ND, go, 0)
        if to_spectral:
            pltpu.make_async_copy(snd.at[k, me], rcv.at[k, z * NS + s], rsem.at[k]).start()
        else:
            pltpu.make_async_copy(snd.at[k, z * NS + s], rcv.at[k, me], rsem.at[k]).start()

    def wait_all(phase, i):
        k = phase * 2 + i
        pltpu.make_async_copy(rcv.at[k], rcv.at[k], rsem.at[k]).wait()

    def window(ref, r):
        return jnp.concatenate(
            [ref[:, g * GROUP + STARTS[r] : g * GROUP + STARTS[r] + WIN] for g in range(4)], axis=0
        )

    def table(r):
        return tab[r].reshape(2 * ORD, WIN)

    def fourier_tiles(data, r, factor, orders=(0, 1)):
        rows_of = tab[r].reshape(2 * ORD, WIN) if len(orders) == 2 else tab[r, orders[0]].reshape(ORD, WIN)
        prod = dot_nt(rows_of, data) * factor
        for n, i in enumerate(orders):
            rows = prod[n * ORD : n * ORD + ORD]
            for pair in range(2):
                lanes = slice(pair * 128, pair * 128 + 128)
                tiles = swap_halves(rows[:ND, lanes], rows[ND:, lanes])
                for m in range(2):
                    scr[i, pl.ds((pair * 2 + m) * 4 + r, ND, stride=LD), :] = tiles[m]

    def pack_send(phase, i):
        snd[phase * 2 + i] = scr[i].reshape(ND, LD, 128).astype(BF)

    def input_order(i):
        for r in range(4):
            fourier_tiles(window(x_v, r), r, 1.0 / math.sqrt(NLON), (i,))
        pack_send(0, i)

    fourier_table(0)
    x_in.wait()
    cot_in.start()
    input_order(0)
    pl.semaphore_wait(barrier, ND - 1)
    start_all(0, 0, True)
    fourier_table(1)
    input_order(1)

    gain_both = gain_ref[...].astype(F32)
    gain_both = jnp.transpose(jnp.concatenate([gain_both, gain_both], axis=0))
    folded = jnp.where(low_half((320, 128)), gain_both[:320], gain_both[320:])
    gfold[...] = folded.reshape(2, GROWS, 128).astype(BF)
    wg[z, core, 0:CD] = w_ref[core, :, 0:128]
    wg[z, core, CD:WROWS] = w_ref[core, :, 128:256]
    wg[z, core, WROWS : WROWS + GROWS] = gfold[core]

    def share_weights(n):
        dz = n % 3 + 1
        tile = wg.at[z, core, pl.ds(pl.multiple_of(n // 3 * 16, 16), 16)]
        pltpu.make_async_remote_copy(
            src_ref=tile, dst_ref=tile, send_sem=wsem.at[0], recv_sem=wrsem.at[dz],
            device_id=(s, (z + dz) % NZ), device_id_type=MESH,
        ).start()

    start_all(0, 1, True, share_weights, 3 * (WROWS + GROWS) // 16)

    order_here = [ords_smem[2 * me + i].astype(F32) for i in range(2)]
    phase_sc = []
    for i in range(2):
        phi = jnp.full((16, 128), 1.0, F32) * (order_here[i] * 0.37)
        turns = jnp.floor(phi * (1.0 / (2.0 * math.pi)) + 0.5)
        phi = (phi - turns * 6.28125) - turns * (2.0 * math.pi - 6.28125)
        phase_sc.append(sincos(phi))

    def with_phase(i, sn, cs):
        sp, cp = phase_sc[i]
        sp, cp = sp[:, :1], cp[:, :1]
        return sn * cp + cs * sp, cs * cp - sn * sp

    def legendre_rows(ref, width, blocks, degree_in_rows):
        odd = (2 * iota((16, width), 1) + 1).astype(F32)
        bs, bc = turn((2 * iota((16, width), 0) + 1).astype(F32) * odd, 4096.0)
        base = [with_phase(i, bs, bc) for i in range(2)]

        def rows(q, carry):
            first = q * 16
            sa, ca = turn((2 * first).astype(F32) * odd[:8], 4096.0)
            sa, ca = jnp.concatenate([sa, sa], axis=0), jnp.concatenate([ca, ca], axis=0)
            degree = first + iota((16, width), 0) if degree_in_rows else iota((16, width), 1)
            for i in range(2):
                sb, cb = base[i]
                value = jnp.where(degree.astype(F32) >= order_here[i], ca * cb - sa * sb, 0.0)
                ref[i, pl.ds(pl.multiple_of(first, 16), 16), :] = value.astype(BF)
            return carry

        lax.fori_loop(0, blocks, rows, 0)

    legendre_rows(leg, NLAT, LMAX // 16, True)
    legendre_rows(legt, LMAX, NLAT // 16, False)

    for dz in range(1, NZ):
        arrived = wg.at[(z + NZ - dz) % NZ, core]
        pltpu.make_async_copy(arrived, arrived, wrsem.at[dz]).wait()
    to_sibling = pltpu.make_async_remote_copy(
        src_ref=wg.at[:, core], dst_ref=wg.at[:, core], send_sem=wsem.at[1], recv_sem=wrsem.at[0],
        device_id=(sibling, z), device_id_type=MESH,
    )
    to_sibling.start()

    def project(phase, i):
        k = phase * 2 + i
        data = jnp.concatenate(
            [rcv[k, zz * NS : zz * NS + NS].reshape(NLAT, 128) for zz in range(NZ)], axis=1
        )
        return dot_nn(leg[i], data) * 0.0625

    def expand(phase, i):
        k = phase * 2 + i
        grid = dot_nn(legt[i], spec[i]) * 0.0625
        for zz in range(NZ):
            part = grid[:, zz * 128 : zz * 128 + 128].reshape(NS, LD, 128)
            snd[k, zz * NS : zz * NS + NS] = part.astype(BF)

    wait_all(0, 0)
    coeffs[0] = project(0, 0).astype(BF)

    to_sibling.wait_recv()
    for zz in range(NZ):
        for u in range(2):
            a = wg[zz, 0, u * CD : u * CD + CD].astype(F32)
            b = wg[zz, 1, u * CD : u * CD + CD].astype(F32)
            top = swap_halves(a, b)
            low = swap_halves(-b, a)
            for n in range(2):
                lanes = slice((2 * u + n) * 128, (2 * u + n) * 128 + 128)
                mat[zz * 128 : zz * 128 + CD, lanes] = top[n].astype(BF)
                mat[zz * 128 + CD : zz * 128 + 128, lanes] = low[n].astype(BF)
        fold = wg[zz, :, WROWS : WROWS + GROWS].astype(F32).reshape(320, 128)
        both = pltpu.roll(fold, 64, 1)
        low = low_half((320, 128))
        gains[0:320, zz * 128 : zz * 128 + 128] = jnp.where(low, fold, both).astype(BF)
        gains[320:640, zz * 128 : zz * 128 + 128] = jnp.where(low, both, fold).astype(BF)

    def mix(i):
        prod = dot_nn(coeffs[i], mat[...])
        mixed[i] = prod
        spec[i] = (gains[...].astype(F32) * prod).astype(BF)
        expand(1, i)
        start_all(1, i, False)

    mix(0)
    wait_all(0, 1)
    coeffs[1] = project(0, 1).astype(BF)
    mix(1)

    def order_rows(r):
        parts = []
        for i in range(2):
            tiles = [scr[i, pl.ds(4 * g + r, ND, stride=LD), :] for g in range(4)]
            pairs = [swap_halves(tiles[0], tiles[1]), swap_halves(tiles[2], tiles[3])]
            parts += [jnp.concatenate([pairs[0][p], pairs[1][p]], axis=1) for p in range(2)]
        return jnp.concatenate(parts, axis=0).astype(BF)

    def unpack(phase, i):
        wait_all(phase, i)
        scr[i] = rcv[phase * 2 + i].astype(F32).reshape(ND * LD, 128)

    def put_window(ref, r, value):
        for g in range(4):
            part = value[g * CD : g * CD + CD]
            lo = g * GROUP + STARTS[r]
            if r > 0:
                first = ref[:, lo : lo + 128].astype(F32) + part[:, :128]
                ref[:, lo : lo + 128] = first.astype(BF)
                ref[:, lo + 128 : lo + WIN] = part[:, 128:].astype(BF)
            else:
                ref[:, lo : lo + WIN] = part.astype(BF)

    cot_in.wait()
    unpack(1, 0)
    unpack(1, 1)
    rows = [order_rows(r) for r in range(4)]
    for r in range(4):
        before = dot_tn(rows[r], table(r)) * 0.0625
        value, slope = gelu_parts(before)
        put_window(out_v, r, value)
        grad = (window(cot_v, r).astype(F32) * slope).astype(BF)
        fourier_tiles(grad, r, 0.0625)
    for i in range(2):
        pack_send(2, i)
        start_all(2, i, True)

    def back(i):
        wait_all(2, i)
        value = project(2, i)
        here = value * mixed[i]
        gsum[...] = here if i == 0 else gsum[...] + here
        spec[i] = (gains[...].astype(F32) * value).astype(BF)
        if i == 0:
            wpart = dot_tn(coeffs[0], spec[0])
            mixed[0, :512] = wpart
        else:
            wpart = dot_tn(coeffs[1], spec[1]) + mixed[0, :512]
            sign = jnp.where(low_half((CD, 128)), 1.0, -1.0)
            for zz in range(NZ):
                for zo in range(NZ):
                    lanes = slice(zo * 128, zo * 128 + 128)
                    up = wpart[zz * 128 : zz * 128 + CD, lanes]
                    down = wpart[zz * 128 + CD : zz * 128 + 128, lanes]
                    redw[zz, zo * CD : zo * CD + CD] = (up + pltpu.roll(down, 64, 1) * sign).astype(BF)
                both = gsum[:, zz * 128 : zz * 128 + 128]
                both = both + pltpu.roll(both, 64, 1)
                redg[zz] = jnp.where(low_half((320, 128)), both[:320], both[320:]).astype(BF)

    def to_inputs(i):
        spec[i] = dot_nt(spec[i], mat[...]).astype(BF)

    back(0)
    to_inputs(0)
    expand(3, 0)
    start_all(3, 0, False)
    back(1)

    @pl.when(core == 0)
    def _():
        pltpu.make_async_remote_copy(
            src_ref=redg, dst_ref=pairg, send_sem=dsem.at[0], recv_sem=drsem.at[0],
            device_id=(sibling, z), device_id_type=MESH,
        ).start()

    @pl.when(core == 1)
    def _():
        pltpu.make_async_remote_copy(
            src_ref=redw, dst_ref=pairw, send_sem=dsem.at[0], recv_sem=drsem.at[0],
            device_id=(sibling, z), device_id_type=MESH,
        ).start()

    to_inputs(1)
    expand(3, 1)

    source = xy * NZ + z

    @pl.when(core == 0)
    def _():
        pltpu.make_async_copy(pairw, pairw, drsem.at[0]).wait()
        pairw[...] = (pairw[...].astype(F32) + redw[...].astype(F32)).astype(BF)

        def go(n, carry):
            t = (source + n * 37) % (NXY * NZ)
            txy, tz = t // NZ, t % NZ
            pltpu.make_async_remote_copy(
                src_ref=pairw.at[tz, pl.ds(pl.multiple_of(txy * WCH, WCH), WCH)], dst_ref=inw.at[source],
                send_sem=dsem.at[1], recv_sem=drsem.at[1], device_id=(txy * 2, tz), device_id_type=MESH,
            ).start()
            return carry

        lax.fori_loop(1, NXY * NZ, go, 0)
        pltpu.make_async_copy(
            pairw.at[z, pl.ds(pl.multiple_of(xy * WCH, WCH), WCH)], inw.at[source], drsem.at[1]
        ).start()

    chunk = (xy * 5 + 7) // 8
    adds_gain = (chunk * 8) // 5 == xy

    @pl.when(core == 1)
    def _():
        pltpu.make_async_copy(pairg, pairg, drsem.at[0]).wait()
        pairg[...] = (pairg[...].astype(F32) + redg[...].astype(F32)).astype(BF)

        def go(n, carry):
            ch, tz = n % NG, (z + n // NG) % NZ
            txy = (ch * 8) // 5

            @pl.when(txy * NZ + tz != source)
            def _():
                pltpu.make_async_remote_copy(
                    src_ref=pairg.at[tz, pl.ds(pl.multiple_of(ch * GCH, GCH), GCH)], dst_ref=ing.at[source],
                    send_sem=dsem.at[2], recv_sem=drsem.at[2], device_id=(txy * 2 + 1, tz), device_id_type=MESH,
                ).start()

            @pl.when(txy * NZ + tz == source)
            def _():
                pltpu.make_async_copy(
                    pairg.at[tz, pl.ds(pl.multiple_of(ch * GCH, GCH), GCH)], ing.at[source], drsem.at[2]
                ).start()

            return carry

        lax.fori_loop(0, NG * NZ, go, 0)

    start_all(3, 1, False)

    def share(mine, fin, at, sem):
        def go(n, carry):
            pltpu.make_async_remote_copy(
                src_ref=mine, dst_ref=fin.at[at], send_sem=dsem.at[sem], recv_sem=drsem.at[sem],
                device_id=((s + n) % NS, z), device_id_type=MESH,
            ).start()
            return carry

        lax.fori_loop(1, NS, go, 0)
        pltpu.make_async_copy(mine, fin.at[at], drsem.at[sem]).start()

    unpack(3, 0)

    @pl.when(core == 0)
    def _():
        pltpu.make_async_copy(inw, inw, drsem.at[1]).wait()
        minew[...] = jnp.sum(inw[...].astype(F32), axis=0).astype(BF)
        share(minew, finw, xy, 3)

    @pl.when(jnp.logical_and(core == 1, adds_gain))
    def _():
        pltpu.make_async_copy(ing, ing, drsem.at[2]).wait()
        mineg[...] = jnp.sum(ing[...].astype(F32), axis=0).astype(BF)
        share(mineg, fing, chunk, 4)

    unpack(3, 1)
    rows = [order_rows(r) for r in range(4)]
    for r in range(4):
        put_window(x_v, r, dot_tn(rows[r], table(r)) * (1.0 / math.sqrt(NLON)))

    pltpu.make_async_copy(finw, finw, drsem.at[3]).wait()
    pltpu.make_async_copy(fing, fing, drsem.at[4]).wait()
    wscale = 1.0 / math.sqrt(ORD * LMAX)
    sums = finw[...].astype(F32).reshape(NZ, CD, 128) * wscale
    for u in range(2):
        pair = swap_halves(sums[2 * u], sums[2 * u + 1])
        for p in range(2):
            wgrad_ref[p, :, u * 128 : u * 128 + 128] = pair[p]
    fold = fing[...].astype(F32).reshape(320, 128) * (1.0 / math.sqrt(ORD))
    ggrad_ref[...] = jnp.transpose(jnp.concatenate([fold, pltpu.roll(fold, 64, 1)], axis=0))[:CD]

    for k in range(8):
        pltpu.make_async_copy(snd.at[k, pl.ds(0, ND - 1)], snd.at[k, pl.ds(0, ND - 1)], ssem.at[k]).wait()
    for dz in range(1, NZ):
        pltpu.make_async_copy(wg.at[z, core], wg.at[z, core], wsem.at[0]).wait()
    to_sibling.wait_send()

    @pl.when(core == 0)
    def _():
        pltpu.make_async_copy(redg, redg, dsem.at[0]).wait()
        others = NXY * NZ - 1
        pltpu.make_async_copy(inw.at[pl.ds(0, others)], inw.at[pl.ds(0, others)], dsem.at[1]).wait()
        pltpu.make_async_copy(sent(finw), sent(finw), dsem.at[3]).wait()
        pltpu.make_async_copy(rest(finw), rest(finw), dsem.at[3]).wait()

    @pl.when(core == 1)
    def _():
        pltpu.make_async_copy(redw, redw, dsem.at[0]).wait()

        @pl.when(adds_gain)
        def _():
            others = NG * NZ - 1
            pltpu.make_async_copy(ing.at[pl.ds(0, others)], ing.at[pl.ds(0, others)], dsem.at[2]).wait()
            for _ in range(3):
                pltpu.make_async_copy(fing, fing, dsem.at[4]).wait()
            pltpu.make_async_copy(mineg, mineg, dsem.at[4]).wait()

        @pl.when(jnp.logical_not(adds_gain))
        def _():
            others = NG * NZ
            pltpu.make_async_copy(ing.at[pl.ds(0, others)], ing.at[pl.ds(0, others)], dsem.at[2]).wait()


def sent(fin):
    return fin.at[pl.ds(0, NXY)]


def rest(fin):
    return fin.at[pl.ds(0, NXY - 1)]


def finish(*refs):
    sem = refs[-1]
    copies = [pltpu.make_async_copy(refs[i], refs[4 + i], sem.at[i]) for i in range(4)]
    for copy in copies:
        copy.start()
    for copy in copies:
        copy.wait()


def body(fields, mixing_weight, degree_gain, cotangent, order_ids):
    cells = fields.shape[2]
    vmem = pl.BlockSpec(memory_space=pltpu.VMEM)
    anyw = pl.BlockSpec(memory_space=pl.ANY)
    smem = pl.BlockSpec(memory_space=pltpu.SMEM)
    shapes = (
        ((CD, cells), BF),
        ((CD, cells), BF),
        ((2, CD, 256), F32),
        ((CD, LMAX), F32),
    )
    results = pl.pallas_call(
        kernel,
        out_shape=tuple(pltpu.VMEM(shape, kind) for shape, kind in shapes),
        in_specs=[anyw, vmem, vmem, anyw, vmem, smem],
        out_specs=(vmem,) * 4,
        scratch_shapes=[
            pltpu.VMEM((CD, cells), BF),
            pltpu.VMEM((4, 2, 2, ND, WIN), BF),
            pltpu.VMEM((2, ND, 384), F32),
            pltpu.VMEM((2, LMAX, NLAT), BF),
            pltpu.VMEM((2, NLAT, LMAX), BF),
            pltpu.VMEM((2, ND * LD, 128), F32),
            pltpu.VMEM((8, ND, LD, 128), BF),
            pltpu.VMEM((8, ND, LD, 128), BF),
            pltpu.VMEM((2, GROWS, 128), BF),
            pltpu.VMEM((NZ, 2, WROWS + GROWS, 128), BF),
            pltpu.VMEM((512, 512), BF),
            pltpu.VMEM((LMAX, 512), BF),
            pltpu.VMEM((LMAX, 512), F32),
            pltpu.VMEM((2, LMAX, 512), F32),
            pltpu.VMEM((2, LMAX, 512), BF),
            pltpu.VMEM((2, LMAX, 512), BF),
            pltpu.VMEM((NZ, 256, 128), BF),
            pltpu.VMEM((NZ, 320, 128), BF),
            pltpu.VMEM((NZ, 256, 128), BF),
            pltpu.VMEM((NZ, 320, 128), BF),
            pltpu.VMEM((NXY * NZ, WCH, 128), BF),
            pltpu.VMEM((NXY * NZ, GCH, 128), BF),
            pltpu.VMEM((WCH, 128), BF),
            pltpu.VMEM((GCH, 128), BF),
            pltpu.VMEM((NXY, WCH, 128), BF),
            pltpu.VMEM((NG, GCH, 128), BF),
            pltpu.SemaphoreType.DMA((2,)),
            pltpu.SemaphoreType.DMA((8,)),
            pltpu.SemaphoreType.DMA((8,)),
            pltpu.SemaphoreType.DMA((2,)),
            pltpu.SemaphoreType.DMA((4,)),
            pltpu.SemaphoreType.DMA((5,)),
            pltpu.SemaphoreType.DMA((5,)),
        ],
        compiler_params=pltpu.CompilerParams(
            collective_id=0, has_side_effects=True, vmem_limit_bytes=50 << 20
        ),
    )(
        fields.reshape(CD, cells), mixing_weight, degree_gain.T, cotangent.reshape(CD, cells),
        order_ids.reshape(1, ORD), order_ids,
    )
    out, fgrad, wgrad, ggrad = pl.pallas_call(
        finish,
        out_shape=tuple(jax.ShapeDtypeStruct(shape, kind) for shape, kind in shapes),
        in_specs=[anyw] * 4,
        out_specs=(anyw,) * 4,
        scratch_shapes=[pltpu.SemaphoreType.DMA((4,))],
        compiler_params=pltpu.CompilerParams(vmem_limit_bytes=1 << 20),
    )(*[pltpu.with_memory_space_constraint(a, pltpu.VMEM) for a in results])
    return out.reshape(1, CD, cells), fgrad.reshape(1, CD, cells), wgrad, ggrad.T


def solution(mesh):
    return jax.shard_map(
        body,
        mesh=mesh,
        in_specs=(
            P(None, "chan", "spatial"),
            P(None, "chan", None),
            P(None, "chan"),
            P(None, "chan", "spatial"),
            P(),
        ),
        out_specs=(
            P(None, "chan", "spatial"),
            P(None, "chan", "spatial"),
            P(None, "chan", None),
            P(None, "chan"),
        ),
        check_vma=False,
    )
```

```python
import math

import jax
import jax.numpy as jnp
from jax import lax
from jax.experimental import pallas as pl
from jax.experimental.pallas import tpu as pltpu
from jax.sharding import PartitionSpec as P

MESH = pl.DeviceIdType.MESH
BF = jnp.bfloat16
F32 = jnp.float32

NLON = 1440
NLAT = 512
LMAX = 640
ORD = 256
NS = 32
NZ = 4
ND = NS * NZ
NXY = NS // 2
CD = 64
LD = 16
GROUP = 4 * NLON
WIN = 1536
STARTS = tuple((NLON * r) // 128 * 128 for r in range(4))
WROWS = 128
GROWS = 160
WCH = 16
GCH = 32
NG = 320 // GCH


def sincos(angle):
    h = angle * 0.5
    y = h * h
    s = y * (-1.0 / 39916800.0) + 1.0 / 362880.0
    s = s * y - 1.0 / 5040.0
    s = s * y + 1.0 / 120.0
    s = s * y - 1.0 / 6.0
    s = (s * y + 1.0) * h
    c = y * (1.0 / 479001600.0) - 1.0 / 3628800.0
    c = c * y + 1.0 / 40320.0
    c = c * y - 1.0 / 720.0
    c = c * y + 1.0 / 24.0
    c = c * y - 0.5
    c = c * y + 1.0
    return 2.0 * s * c, 1.0 - 2.0 * s * s


def turn(steps, period):
    rest = steps - period * jnp.floor(steps * (1.0 / period) + 0.5)
    return sincos(rest * (2.0 * math.pi / period))


def iota(shape, dim):
    return lax.broadcasted_iota(jnp.int32, shape, dim)


def gelu_parts(v):
    cdf = 0.5 * (1.0 + lax.erf(v * 0.7071067811865476))
    density = jnp.exp(-0.5 * v * v) * 0.3989422804014327
    return v * cdf, cdf + v * density


def low_half(shape):
    return iota(shape, 1) < 64


def swap_halves(a, b):
    low = low_half(a.shape)
    return (
        jnp.where(low, a, pltpu.roll(b, 64, 1)),
        jnp.where(low, pltpu.roll(a, 64, 1), b),
    )


def dot_nn(a, b):
    return lax.dot_general(a, b, (((1,), (0,)), ((), ())), preferred_element_type=F32)


def dot_nt(a, b):
    return lax.dot_general(a, b, (((1,), (1,)), ((), ())), preferred_element_type=F32)


def dot_tn(a, b):
    return lax.dot_general(a, b, (((0,), (0,)), ((), ())), preferred_element_type=F32)


def kernel(
    x_hbm, w_ref, gain_ref, cot_hbm, ords_ref, ords_smem,
    out_v, x_v, wgrad_ref, ggrad_ref,
    cot_v, tab, trig, leg, legt, scr, partial, grads,
    snd, rcv, gfold, wg, mat, gains,
    gsum, mixed, coeffs, spec, redw, redg, pairw, pairg, inw, ing, minew, mineg, finw, fing,
    in_sem, ssem, rsem, wsem, wrsem, dsem, drsem,
):
    s = lax.axis_index("spatial")
    z = lax.axis_index("chan")
    me = s * NZ + z
    core = s % 2
    xy = s // 2
    sibling = s + 1 - 2 * core
    barrier = pltpu.get_barrier_semaphore()

    def greet(i, carry):
        t = (me + i * 37) % ND
        pl.semaphore_signal(barrier, inc=1, device_id=(t // NZ, t % NZ), device_id_type=MESH)
        return carry

    lax.fori_loop(1, ND, greet, 0)
    x_in = pltpu.make_async_copy(x_hbm, x_v, in_sem.at[0])
    x_in.start()
    cot_in = pltpu.make_async_copy(cot_hbm, cot_v, in_sem.at[1])

    def fourier_table(i):
        row = jnp.broadcast_to(ords_ref[...].astype(F32), (ND, ORD))
        picked = iota((ND, ORD), 1) == 2 * iota((ND, ORD), 0) + i
        order_col = jnp.sum(jnp.where(picked, row, 0.0), axis=1, keepdims=True)
        lane = iota((ND, 384), 1)
        step = jnp.where(lane < 256, lane - 128, (lane - 256) * 128).astype(F32)
        sin_all, cos_all = turn(order_col * step, float(NLON))
        trig[0] = sin_all
        trig[1] = cos_all

        def some_rows(b, carry):
            rows = pl.ds(pl.multiple_of(b * 64, 64), 64)
            sin_row = trig[0, rows, :]
            cos_row = trig[1, rows, :]
            at = iota((64, 128), 1)
            shifted = []
            for r in range(4):
                lo = 128 - 32 * r
                shifted.append((sin_row[:, lo : lo + 128], cos_row[:, lo : lo + 128]))
            for q in range(12):
                sa = jnp.broadcast_to(sin_row[:, 256 + q : 257 + q], (64, 128))
                ca = jnp.broadcast_to(cos_row[:, 256 + q : 257 + q], (64, 128))
                for r in range(4):
                    sb, cb = shifted[r]
                    even = ca * cb - sa * sb
                    odd = -(sa * cb + ca * sb)
                    if q == 0 and r > 0:
                        even = jnp.where(at < 32 * r, 0.0, even)
                        odd = jnp.where(at < 32 * r, 0.0, odd)
                    if q == 11 and r < 3:
                        even = jnp.where(at >= 32 * r + 32, 0.0, even)
                        odd = jnp.where(at >= 32 * r + 32, 0.0, odd)
                    tab[r, i, 0, rows, q * 128 : q * 128 + 128] = even.astype(BF)
                    tab[r, i, 1, rows, q * 128 : q * 128 + 128] = odd.astype(BF)
            return carry

        lax.fori_loop(0, ND // 64, some_rows, 0)

    def start_all(phase, i, to_spectral, beside=None, count=0):
        k = phase * 2 + i

        def go(n, carry):
            t = (me + n * 37) % ND
            ts, tz = t // NZ, t % NZ
            if to_spectral:
                src, dst = snd.at[k, t], rcv.at[k, z * NS + s]
            else:
                src, dst = snd.at[k, tz * NS + ts], rcv.at[k, me]
            pltpu.make_async_remote_copy(
                src_ref=src, dst_ref=dst, send_sem=ssem.at[k], recv_sem=rsem.at[k],
                device_id=(ts, tz), device_id_type=MESH,
            ).start()
            return carry

        def go_both(n, carry):
            beside(n - 1)
            return go(n, carry)

        if count:
            lax.fori_loop(1, 1 + count, go_both, 0)
        lax.fori_loop(1 + count, ND, go, 0)
        if to_spectral:
            pltpu.make_async_copy(snd.at[k, me], rcv.at[k, z * NS + s], rsem.at[k]).start()
        else:
            pltpu.make_async_copy(snd.at[k, z * NS + s], rcv.at[k, me], rsem.at[k]).start()

    def wait_all(phase, i):
        k = phase * 2 + i
        pltpu.make_async_copy(rcv.at[k], rcv.at[k], rsem.at[k]).wait()

    def window(ref, r):
        return jnp.concatenate(
            [ref[:, g * GROUP + STARTS[r] : g * GROUP + STARTS[r] + WIN] for g in range(4)], axis=0
        )

    def fourier_tiles(i, data, r, factor):
        prod = dot_nt(tab[r, i].reshape(ORD, WIN), data) * factor
        for pair in range(2):
            lanes = slice(pair * 128, pair * 128 + 128)
            tiles = swap_halves(prod[:ND, lanes], prod[ND:, lanes])
            for m in range(2):
                scr[i, pl.ds((pair * 2 + m) * 4 + r, ND, stride=LD), :] = tiles[m]

    def pack_send(phase, i):
        snd[phase * 2 + i] = scr[i].reshape(ND, LD, 128).astype(BF)

    def input_order(i):
        for r in range(4):
            fourier_tiles(i, window(x_v, r), r, 1.0 / math.sqrt(NLON))
        pack_send(0, i)

    gain_both = gain_ref[...].astype(F32)
    gain_both = jnp.transpose(jnp.concatenate([gain_both, gain_both], axis=0))
    folded = jnp.where(low_half((320, 128)), gain_both[:320], gain_both[320:])
    gfold[...] = folded.reshape(2, GROWS, 128).astype(BF)
    wg[z, core, 0:CD] = w_ref[core, :, 0:128]
    wg[z, core, CD:WROWS] = w_ref[core, :, 128:256]
    wg[z, core, WROWS : WROWS + GROWS] = gfold[core]

    def share_weights(n):
        dz = n % 3 + 1
        tile = wg.at[z, core, pl.ds(pl.multiple_of(n // 3 * 16, 16), 16)]
        pltpu.make_async_remote_copy(
            src_ref=tile, dst_ref=tile, send_sem=wsem.at[0], recv_sem=wrsem.at[dz],
            device_id=(s, (z + dz) % NZ), device_id_type=MESH,
        ).start()

    fourier_table(0)
    x_in.wait()
    cot_in.start()
    input_order(0)
    pl.semaphore_wait(barrier, ND - 1)
    start_all(0, 0, True, share_weights, 3 * (WROWS + GROWS) // 16)
    fourier_table(1)
    input_order(1)

    start_all(0, 1, True)

    order_here = [ords_smem[2 * me + i].astype(F32) for i in range(2)]
    phase_sc = []
    for i in range(2):
        phi = jnp.full((16, 128), 1.0, F32) * (order_here[i] * 0.37)
        turns = jnp.floor(phi * (1.0 / (2.0 * math.pi)) + 0.5)
        phi = (phi - turns * 6.28125) - turns * (2.0 * math.pi - 6.28125)
        phase_sc.append(sincos(phi))

    def with_phase(i, sn, cs):
        sp, cp = phase_sc[i]
        sp, cp = sp[:, :1], cp[:, :1]
        return sn * cp + cs * sp, cs * cp - sn * sp

    def legendre_rows(ref, width, blocks, degree_in_rows):
        odd = (2 * iota((16, width), 1) + 1).astype(F32)
        bs, bc = turn((2 * iota((16, width), 0) + 1).astype(F32) * odd, 4096.0)
        base = [with_phase(i, bs, bc) for i in range(2)]

        def rows(q, carry):
            first = q * 16
            sa, ca = turn((2 * first).astype(F32) * odd[:8], 4096.0)
            sa, ca = jnp.concatenate([sa, sa], axis=0), jnp.concatenate([ca, ca], axis=0)
            degree = first + iota((16, width), 0) if degree_in_rows else iota((16, width), 1)
            for i in range(2):
                sb, cb = base[i]
                value = jnp.where(degree.astype(F32) >= order_here[i], ca * cb - sa * sb, 0.0)
                ref[i, pl.ds(pl.multiple_of(first, 16), 16), :] = value.astype(BF)
            return carry

        lax.fori_loop(0, blocks, rows, 0)

    legendre_rows(leg, NLAT, LMAX // 16, True)
    legendre_rows(legt, LMAX, NLAT // 16, False)

    for dz in range(1, NZ):
        arrived = wg.at[(z + NZ - dz) % NZ, core]
        pltpu.make_async_copy(arrived, arrived, wrsem.at[dz]).wait()
    to_sibling = pltpu.make_async_remote_copy(
        src_ref=wg.at[:, core], dst_ref=wg.at[:, core], send_sem=wsem.at[1], recv_sem=wrsem.at[0],
        device_id=(sibling, z), device_id_type=MESH,
    )
    to_sibling.start()

    def project(phase, i):
        k = phase * 2 + i
        data = jnp.concatenate(
            [rcv[k, zz * NS : zz * NS + NS].reshape(NLAT, 128) for zz in range(NZ)], axis=1
        )
        return dot_nn(leg[i], data) * 0.0625

    def expand(phase, i):
        k = phase * 2 + i
        grid = dot_nn(legt[i], spec[i]) * 0.0625
        for zz in range(NZ):
            part = grid[:, zz * 128 : zz * 128 + 128].reshape(NS, LD, 128)
            snd[k, zz * NS : zz * NS + NS] = part.astype(BF)

    wait_all(0, 0)
    coeffs[0] = project(0, 0).astype(BF)

    to_sibling.wait_recv()
    for zz in range(NZ):
        for u in range(2):
            a = wg[zz, 0, u * CD : u * CD + CD].astype(F32)
            b = wg[zz, 1, u * CD : u * CD + CD].astype(F32)
            top = swap_halves(a, b)
            low = swap_halves(-b, a)
            for n in range(2):
                lanes = slice((2 * u + n) * 128, (2 * u + n) * 128 + 128)
                mat[zz * 128 : zz * 128 + CD, lanes] = top[n].astype(BF)
                mat[zz * 128 + CD : zz * 128 + 128, lanes] = low[n].astype(BF)
        fold = wg[zz, :, WROWS : WROWS + GROWS].astype(F32).reshape(320, 128)
        both = pltpu.roll(fold, 64, 1)
        low = low_half((320, 128))
        gains[0:320, zz * 128 : zz * 128 + 128] = jnp.where(low, fold, both).astype(BF)
        gains[320:640, zz * 128 : zz * 128 + 128] = jnp.where(low, both, fold).astype(BF)

    def mix(i):
        prod = dot_nn(coeffs[i], mat[...])
        mixed[i] = prod
        spec[i] = (gains[...].astype(F32) * prod).astype(BF)
        expand(1, i)
        start_all(1, i, False)

    mix(0)
    wait_all(0, 1)
    coeffs[1] = project(0, 1).astype(BF)
    mix(1)

    def order_rows(i, r):
        tiles = [scr[i, pl.ds(4 * g + r, ND, stride=LD), :] for g in range(4)]
        pairs = [swap_halves(tiles[0], tiles[1]), swap_halves(tiles[2], tiles[3])]
        parts = [jnp.concatenate([pairs[0][p], pairs[1][p]], axis=1) for p in range(2)]
        return jnp.concatenate(parts, axis=0).astype(BF)

    def unpack(phase, i):
        wait_all(phase, i)
        scr[i] = rcv[phase * 2 + i].astype(F32).reshape(ND * LD, 128)

    def grid_part(i, r):
        return dot_tn(order_rows(i, r), tab[r, i].reshape(ORD, WIN))

    def first_part(phase):
        unpack(phase, 0)
        for r in range(4):
            partial[r] = grid_part(0, r)

    def put_window(ref, r, value):
        for g in range(4):
            part = value[g * CD : g * CD + CD]
            lo = g * GROUP + STARTS[r]
            if r > 0:
                first = ref[:, lo : lo + 128].astype(F32) + part[:, :128]
                ref[:, lo : lo + 128] = first.astype(BF)
                ref[:, lo + 128 : lo + WIN] = part[:, 128:].astype(BF)
            else:
                ref[:, lo : lo + WIN] = part.astype(BF)

    cot_in.wait()
    first_part(1)
    unpack(1, 1)
    for r in range(4):
        before = (partial[r] + grid_part(1, r)) * 0.0625
        value, slope = gelu_parts(before)
        put_window(out_v, r, value)
        grads[r] = (window(cot_v, r).astype(F32) * slope).astype(BF)
        fourier_tiles(0, grads[r], r, 0.0625)
    pack_send(2, 0)
    start_all(2, 0, True)
    for r in range(4):
        fourier_tiles(1, grads[r], r, 0.0625)
    pack_send(2, 1)
    start_all(2, 1, True)

    def back(i):
        wait_all(2, i)
        value = project(2, i)
        here = value * mixed[i]
        gsum[...] = here if i == 0 else gsum[...] + here
        spec[i] = (gains[...].astype(F32) * value).astype(BF)
        if i == 0:
            wpart = dot_tn(coeffs[0], spec[0])
            mixed[0, :512] = wpart
        else:
            wpart = dot_tn(coeffs[1], spec[1]) + mixed[0, :512]
            sign = jnp.where(low_half((CD, 128)), 1.0, -1.0)
            for zz in range(NZ):
                for zo in range(NZ):
                    lanes = slice(zo * 128, zo * 128 + 128)
                    up = wpart[zz * 128 : zz * 128 + CD, lanes]
                    down = wpart[zz * 128 + CD : zz * 128 + 128, lanes]
                    redw[zz, zo * CD : zo * CD + CD] = (up + pltpu.roll(down, 64, 1) * sign).astype(BF)
                both = gsum[:, zz * 128 : zz * 128 + 128]
                both = both + pltpu.roll(both, 64, 1)
                redg[zz] = jnp.where(low_half((320, 128)), both[:320], both[320:]).astype(BF)

    def to_inputs(i):
        spec[i] = dot_nt(spec[i], mat[...]).astype(BF)

    back(0)
    to_inputs(0)
    expand(3, 0)
    start_all(3, 0, False)
    back(1)

    @pl.when(core == 0)
    def _():
        pltpu.make_async_remote_copy(
            src_ref=redg, dst_ref=pairg, send_sem=dsem.at[0], recv_sem=drsem.at[0],
            device_id=(sibling, z), device_id_type=MESH,
        ).start()

    @pl.when(core == 1)
    def _():
        pltpu.make_async_remote_copy(
            src_ref=redw, dst_ref=pairw, send_sem=dsem.at[0], recv_sem=drsem.at[0],
            device_id=(sibling, z), device_id_type=MESH,
        ).start()

    to_inputs(1)
    expand(3, 1)

    source = xy * NZ + z

    @pl.when(core == 0)
    def _():
        pltpu.make_async_copy(pairw, pairw, drsem.at[0]).wait()
        pairw[...] = (pairw[...].astype(F32) + redw[...].astype(F32)).astype(BF)

        def go(n, carry):
            t = (source + n * 37) % (NXY * NZ)
            txy, tz = t // NZ, t % NZ
            pltpu.make_async_remote_copy(
                src_ref=pairw.at[tz, pl.ds(pl.multiple_of(txy * WCH, WCH), WCH)], dst_ref=inw.at[source],
                send_sem=dsem.at[1], recv_sem=drsem.at[1], device_id=(txy * 2, tz), device_id_type=MESH,
            ).start()
            return carry

        lax.fori_loop(1, NXY * NZ, go, 0)
        pltpu.make_async_copy(
            pairw.at[z, pl.ds(pl.multiple_of(xy * WCH, WCH), WCH)], inw.at[source], drsem.at[1]
        ).start()

    chunk = (xy * 5 + 7) // 8
    adds_gain = (chunk * 8) // 5 == xy

    @pl.when(core == 1)
    def _():
        pltpu.make_async_copy(pairg, pairg, drsem.at[0]).wait()
        pairg[...] = (pairg[...].astype(F32) + redg[...].astype(F32)).astype(BF)

        def go(n, carry):
            ch, tz = n % NG, (z + n // NG) % NZ
            txy = (ch * 8) // 5

            @pl.when(txy * NZ + tz != source)
            def _():
                pltpu.make_async_remote_copy(
                    src_ref=pairg.at[tz, pl.ds(pl.multiple_of(ch * GCH, GCH), GCH)], dst_ref=ing.at[source],
                    send_sem=dsem.at[2], recv_sem=drsem.at[2], device_id=(txy * 2 + 1, tz), device_id_type=MESH,
                ).start()

            @pl.when(txy * NZ + tz == source)
            def _():
                pltpu.make_async_copy(
                    pairg.at[tz, pl.ds(pl.multiple_of(ch * GCH, GCH), GCH)], ing.at[source], drsem.at[2]
                ).start()

            return carry

        lax.fori_loop(0, NG * NZ, go, 0)

    start_all(3, 1, False)

    def share(mine, fin, at, sem):
        def go(n, carry):
            pltpu.make_async_remote_copy(
                src_ref=mine, dst_ref=fin.at[at], send_sem=dsem.at[sem], recv_sem=drsem.at[sem],
                device_id=((s + n) % NS, z), device_id_type=MESH,
            ).start()
            return carry

        lax.fori_loop(1, NS, go, 0)
        pltpu.make_async_copy(mine, fin.at[at], drsem.at[sem]).start()

    first_part(3)

    @pl.when(core == 0)
    def _():
        pltpu.make_async_copy(inw, inw, drsem.at[1]).wait()
        minew[...] = jnp.sum(inw[...].astype(F32), axis=0).astype(BF)
        share(minew, finw, xy, 3)

    @pl.when(jnp.logical_and(core == 1, adds_gain))
    def _():
        pltpu.make_async_copy(ing, ing, drsem.at[2]).wait()
        mineg[...] = jnp.sum(ing[...].astype(F32), axis=0).astype(BF)
        share(mineg, fing, chunk, 4)

    unpack(3, 1)
    for r in range(4):
        put_window(x_v, r, (partial[r] + grid_part(1, r)) * (1.0 / math.sqrt(NLON)))

    pltpu.make_async_copy(finw, finw, drsem.at[3]).wait()
    pltpu.make_async_copy(fing, fing, drsem.at[4]).wait()
    wscale = 1.0 / math.sqrt(ORD * LMAX)
    sums = finw[...].astype(F32).reshape(NZ, CD, 128) * wscale
    for u in range(2):
        pair = swap_halves(sums[2 * u], sums[2 * u + 1])
        for p in range(2):
            wgrad_ref[p, :, u * 128 : u * 128 + 128] = pair[p]
    fold = fing[...].astype(F32).reshape(320, 128) * (1.0 / math.sqrt(ORD))
    ggrad_ref[...] = jnp.transpose(jnp.concatenate([fold, pltpu.roll(fold, 64, 1)], axis=0))[:CD]

    for k in range(8):
        pltpu.make_async_copy(snd.at[k, pl.ds(0, ND - 1)], snd.at[k, pl.ds(0, ND - 1)], ssem.at[k]).wait()
    for dz in range(1, NZ):
        pltpu.make_async_copy(wg.at[z, core], wg.at[z, core], wsem.at[0]).wait()
    to_sibling.wait_send()

    @pl.when(core == 0)
    def _():
        pltpu.make_async_copy(redg, redg, dsem.at[0]).wait()
        others = NXY * NZ - 1
        pltpu.make_async_copy(inw.at[pl.ds(0, others)], inw.at[pl.ds(0, others)], dsem.at[1]).wait()
        pltpu.make_async_copy(sent(finw), sent(finw), dsem.at[3]).wait()
        pltpu.make_async_copy(rest(finw), rest(finw), dsem.at[3]).wait()

    @pl.when(core == 1)
    def _():
        pltpu.make_async_copy(redw, redw, dsem.at[0]).wait()

        @pl.when(adds_gain)
        def _():
            others = NG * NZ - 1
            pltpu.make_async_copy(ing.at[pl.ds(0, others)], ing.at[pl.ds(0, others)], dsem.at[2]).wait()
            for _ in range(3):
                pltpu.make_async_copy(fing, fing, dsem.at[4]).wait()
            pltpu.make_async_copy(mineg, mineg, dsem.at[4]).wait()

        @pl.when(jnp.logical_not(adds_gain))
        def _():
            others = NG * NZ
            pltpu.make_async_copy(ing.at[pl.ds(0, others)], ing.at[pl.ds(0, others)], dsem.at[2]).wait()


def sent(fin):
    return fin.at[pl.ds(0, NXY)]


def rest(fin):
    return fin.at[pl.ds(0, NXY - 1)]


def finish(*refs):
    sem = refs[-1]
    copies = [pltpu.make_async_copy(refs[i], refs[4 + i], sem.at[i]) for i in range(4)]
    for copy in copies:
        copy.start()
    for copy in copies:
        copy.wait()


def body(fields, mixing_weight, degree_gain, cotangent, order_ids):
    cells = fields.shape[2]
    vmem = pl.BlockSpec(memory_space=pltpu.VMEM)
    anyw = pl.BlockSpec(memory_space=pl.ANY)
    smem = pl.BlockSpec(memory_space=pltpu.SMEM)
    shapes = (
        ((CD, cells), BF),
        ((CD, cells), BF),
        ((2, CD, 256), F32),
        ((CD, LMAX), F32),
    )
    results = pl.pallas_call(
        kernel,
        out_shape=tuple(pltpu.VMEM(shape, kind) for shape, kind in shapes),
        in_specs=[anyw, vmem, vmem, anyw, vmem, smem],
        out_specs=(vmem,) * 4,
        scratch_shapes=[
            pltpu.VMEM((CD, cells), BF),
            pltpu.VMEM((4, 2, 2, ND, WIN), BF),
            pltpu.VMEM((2, ND, 384), F32),
            pltpu.VMEM((2, LMAX, NLAT), BF),
            pltpu.VMEM((2, NLAT, LMAX), BF),
            pltpu.VMEM((2, ND * LD, 128), F32),
            pltpu.VMEM((4, 256, WIN), F32),
            pltpu.VMEM((4, 256, WIN), BF),
            pltpu.VMEM((8, ND, LD, 128), BF),
            pltpu.VMEM((8, ND, LD, 128), BF),
            pltpu.VMEM((2, GROWS, 128), BF),
            pltpu.VMEM((NZ, 2, WROWS + GROWS, 128), BF),
            pltpu.VMEM((512, 512), BF),
            pltpu.VMEM((LMAX, 512), BF),
            pltpu.VMEM((LMAX, 512), F32),
            pltpu.VMEM((2, LMAX, 512), F32),
            pltpu.VMEM((2, LMAX, 512), BF),
            pltpu.VMEM((2, LMAX, 512), BF),
            pltpu.VMEM((NZ, 256, 128), BF),
            pltpu.VMEM((NZ, 320, 128), BF),
            pltpu.VMEM((NZ, 256, 128), BF),
            pltpu.VMEM((NZ, 320, 128), BF),
            pltpu.VMEM((NXY * NZ, WCH, 128), BF),
            pltpu.VMEM((NXY * NZ, GCH, 128), BF),
            pltpu.VMEM((WCH, 128), BF),
            pltpu.VMEM((GCH, 128), BF),
            pltpu.VMEM((NXY, WCH, 128), BF),
            pltpu.VMEM((NG, GCH, 128), BF),
            pltpu.SemaphoreType.DMA((2,)),
            pltpu.SemaphoreType.DMA((8,)),
            pltpu.SemaphoreType.DMA((8,)),
            pltpu.SemaphoreType.DMA((2,)),
            pltpu.SemaphoreType.DMA((4,)),
            pltpu.SemaphoreType.DMA((5,)),
            pltpu.SemaphoreType.DMA((5,)),
        ],
        compiler_params=pltpu.CompilerParams(
            collective_id=0, has_side_effects=True, vmem_limit_bytes=50 << 20
        ),
    )(
        fields.reshape(CD, cells), mixing_weight, degree_gain.T, cotangent.reshape(CD, cells),
        order_ids.reshape(1, ORD), order_ids,
    )
    out, fgrad, wgrad, ggrad = pl.pallas_call(
        finish,
        out_shape=tuple(jax.ShapeDtypeStruct(shape, kind) for shape, kind in shapes),
        in_specs=[anyw] * 4,
        out_specs=(anyw,) * 4,
        scratch_shapes=[pltpu.SemaphoreType.DMA((4,))],
        compiler_params=pltpu.CompilerParams(vmem_limit_bytes=1 << 20),
    )(*[pltpu.with_memory_space_constraint(a, pltpu.VMEM) for a in results])
    return out.reshape(1, CD, cells), fgrad.reshape(1, CD, cells), wgrad, ggrad.T


def solution(mesh):
    return jax.shard_map(
        body,
        mesh=mesh,
        in_specs=(
            P(None, "chan", "spatial"),
            P(None, "chan", None),
            P(None, "chan"),
            P(None, "chan", "spatial"),
            P(),
        ),
        out_specs=(
            P(None, "chan", "spatial"),
            P(None, "chan", "spatial"),
            P(None, "chan", None),
            P(None, "chan"),
        ),
        check_vma=False,
    )
```

```python
import math

import jax
import jax.numpy as jnp
from jax import lax
from jax.experimental import pallas as pl
from jax.experimental.pallas import tpu as pltpu
from jax.sharding import PartitionSpec as P

MESH = pl.DeviceIdType.MESH
BF = jnp.bfloat16
F32 = jnp.float32

NLON = 1440
NLAT = 512
LMAX = 640
ORD = 256
NS = 32
NZ = 4
ND = NS * NZ
NXY = NS // 2
CD = 64
LD = 16
GROUP = 4 * NLON
WIN = 1536
STARTS = tuple((NLON * r) // 128 * 128 for r in range(4))
WROWS = 128
GROWS = 160
WCH = 16
GCH = 32
NG = 320 // GCH


def sincos(angle):
    h = angle * 0.5
    y = h * h
    s = y * (-1.0 / 39916800.0) + 1.0 / 362880.0
    s = s * y - 1.0 / 5040.0
    s = s * y + 1.0 / 120.0
    s = s * y - 1.0 / 6.0
    s = (s * y + 1.0) * h
    c = y * (1.0 / 479001600.0) - 1.0 / 3628800.0
    c = c * y + 1.0 / 40320.0
    c = c * y - 1.0 / 720.0
    c = c * y + 1.0 / 24.0
    c = c * y - 0.5
    c = c * y + 1.0
    return 2.0 * s * c, 1.0 - 2.0 * s * s


def turn(steps, period):
    rest = steps - period * jnp.floor(steps * (1.0 / period) + 0.5)
    return sincos(rest * (2.0 * math.pi / period))


def iota(shape, dim):
    return lax.broadcasted_iota(jnp.int32, shape, dim)


def gelu_parts(v):
    cdf = 0.5 * (1.0 + lax.erf(v * 0.7071067811865476))
    density = jnp.exp(-0.5 * v * v) * 0.3989422804014327
    return v * cdf, cdf + v * density


def low_half(shape):
    return iota(shape, 1) < 64


def swap_halves(a, b):
    low = low_half(a.shape)
    return (
        jnp.where(low, a, pltpu.roll(b, 64, 1)),
        jnp.where(low, pltpu.roll(a, 64, 1), b),
    )


def dot_nn(a, b):
    return lax.dot_general(a, b, (((1,), (0,)), ((), ())), preferred_element_type=F32)


def dot_nt(a, b):
    return lax.dot_general(a, b, (((1,), (1,)), ((), ())), preferred_element_type=F32)


def dot_tn(a, b):
    return lax.dot_general(a, b, (((0,), (0,)), ((), ())), preferred_element_type=F32)


def kernel(
    x_hbm, w_ref, gain_ref, cot_hbm, ords_ref, ords_smem,
    out_v, x_v, wgrad_ref, ggrad_ref,
    cot_v, tab, trig, leg, legt, scr, partial, grads,
    snd, rcv, gfold, wg, mat, gains,
    gsum, mixed, coeffs, spec, redw, redg, pairw, pairg, inw, ing, minew, mineg, finw, fing,
    in_sem, ssem, rsem, wsem, wrsem, dsem, drsem,
):
    s = lax.axis_index("spatial")
    z = lax.axis_index("chan")
    me = s * NZ + z
    core = s % 2
    xy = s // 2
    sibling = s + 1 - 2 * core
    barrier = pltpu.get_barrier_semaphore()

    x_in = pltpu.make_async_copy(x_hbm, x_v, in_sem.at[0])
    x_in.start()

    def greet(i, carry):
        t = (me + i * 37) % ND
        pl.semaphore_signal(barrier, inc=1, device_id=(t // NZ, t % NZ), device_id_type=MESH)
        return carry

    lax.fori_loop(1, ND, greet, 0)
    cot_in = pltpu.make_async_copy(cot_hbm, cot_v, in_sem.at[1])

    def fourier_table(i):
        row = jnp.broadcast_to(ords_ref[...].astype(F32), (ND, ORD))
        picked = iota((ND, ORD), 1) == 2 * iota((ND, ORD), 0) + i
        order_col = jnp.sum(jnp.where(picked, row, 0.0), axis=1, keepdims=True)
        lane = iota((ND, 384), 1)
        step = jnp.where(lane < 256, lane - 128, (lane - 256) * 128).astype(F32)
        sin_all, cos_all = turn(order_col * step, float(NLON))
        trig[0] = sin_all
        trig[1] = cos_all

        def some_rows(b, carry):
            rows = pl.ds(pl.multiple_of(b * 64, 64), 64)
            sin_row = trig[0, rows, :]
            cos_row = trig[1, rows, :]
            at = iota((64, 128), 1)
            shifted = []
            for r in range(4):
                lo = 128 - 32 * r
                shifted.append((sin_row[:, lo : lo + 128], cos_row[:, lo : lo + 128]))
            for q in range(12):
                sa = jnp.broadcast_to(sin_row[:, 256 + q : 257 + q], (64, 128))
                ca = jnp.broadcast_to(cos_row[:, 256 + q : 257 + q], (64, 128))
                for r in range(4):
                    sb, cb = shifted[r]
                    even = ca * cb - sa * sb
                    odd = -(sa * cb + ca * sb)
                    if q == 0 and r > 0:
                        even = jnp.where(at < 32 * r, 0.0, even)
                        odd = jnp.where(at < 32 * r, 0.0, odd)
                    if q == 11 and r < 3:
                        even = jnp.where(at >= 32 * r + 32, 0.0, even)
                        odd = jnp.where(at >= 32 * r + 32, 0.0, odd)
                    tab[r, i, 0, rows, q * 128 : q * 128 + 128] = even.astype(BF)
                    tab[r, i, 1, rows, q * 128 : q * 128 + 128] = odd.astype(BF)
            return carry

        lax.fori_loop(0, ND // 64, some_rows, 0)

    def start_all(phase, i, to_spectral, beside=None, count=0):
        k = phase * 2 + i

        def go(n, carry):
            t = (me + n * 37) % ND
            ts, tz = t // NZ, t % NZ
            if to_spectral:
                src, dst = snd.at[k, t], rcv.at[k, z * NS + s]
            else:
                src, dst = snd.at[k, tz * NS + ts], rcv.at[k, me]
            pltpu.make_async_remote_copy(
                src_ref=src, dst_ref=dst, send_sem=ssem.at[k], recv_sem=rsem.at[k],
                device_id=(ts, tz), device_id_type=MESH,
            ).start()
            return carry

        def go_both(n, carry):
            beside(n - 1)
            return go(n, carry)

        if count:
            lax.fori_loop(1, 1 + count, go_both, 0)
        lax.fori_loop(1 + count, ND, go, 0)
        if to_spectral:
            pltpu.make_async_copy(snd.at[k, me], rcv.at[k, z * NS + s], rsem.at[k]).start()
        else:
            pltpu.make_async_copy(snd.at[k, z * NS + s], rcv.at[k, me], rsem.at[k]).start()

    def wait_all(phase, i):
        k = phase * 2 + i
        pltpu.make_async_copy(rcv.at[k], rcv.at[k], rsem.at[k]).wait()

    def window(ref, r):
        return jnp.concatenate(
            [ref[:, g * GROUP + STARTS[r] : g * GROUP + STARTS[r] + WIN] for g in range(4)], axis=0
        )

    def fourier_tiles(i, data, r, factor):
        prod = dot_nt(tab[r, i].reshape(ORD, WIN), data) * factor
        for pair in range(2):
            lanes = slice(pair * 128, pair * 128 + 128)
            tiles = swap_halves(prod[:ND, lanes], prod[ND:, lanes])
            for m in range(2):
                scr[i, pl.ds((pair * 2 + m) * 4 + r, ND, stride=LD), :] = tiles[m]

    def pack_send(phase, i):
        snd[phase * 2 + i] = scr[i].reshape(ND, LD, 128).astype(BF)

    def input_order(i):
        for r in range(4):
            fourier_tiles(i, window(x_v, r), r, 1.0 / math.sqrt(NLON))
        pack_send(0, i)

    gain_both = gain_ref[...].astype(F32)
    gain_both = jnp.transpose(jnp.concatenate([gain_both, gain_both], axis=0))
    folded = jnp.where(low_half((320, 128)), gain_both[:320], gain_both[320:])
    gfold[...] = folded.reshape(2, GROWS, 128).astype(BF)
    wg[z, core, 0:CD] = w_ref[core, :, 0:128]
    wg[z, core, CD:WROWS] = w_ref[core, :, 128:256]
    wg[z, core, WROWS : WROWS + GROWS] = gfold[core]

    def share_weights(n):
        dz = n % 3 + 1
        tile = wg.at[z, core, pl.ds(pl.multiple_of(n // 3 * 16, 16), 16)]
        pltpu.make_async_remote_copy(
            src_ref=tile, dst_ref=tile, send_sem=wsem.at[0], recv_sem=wrsem.at[dz],
            device_id=(s, (z + dz) % NZ), device_id_type=MESH,
        ).start()

    fourier_table(0)
    x_in.wait()
    cot_in.start()
    input_order(0)
    pl.semaphore_wait(barrier, ND - 1)
    start_all(0, 0, True, share_weights, 3 * (WROWS + GROWS) // 16)
    fourier_table(1)
    input_order(1)

    start_all(0, 1, True)

    order_here = [ords_smem[2 * me + i].astype(F32) for i in range(2)]
    phase_sc = []
    for i in range(2):
        phi = jnp.full((16, 128), 1.0, F32) * (order_here[i] * 0.37)
        turns = jnp.floor(phi * (1.0 / (2.0 * math.pi)) + 0.5)
        phi = (phi - turns * 6.28125) - turns * (2.0 * math.pi - 6.28125)
        phase_sc.append(sincos(phi))

    def with_phase(i, sn, cs):
        sp, cp = phase_sc[i]
        sp, cp = sp[:, :1], cp[:, :1]
        return sn * cp + cs * sp, cs * cp - sn * sp

    def legendre_rows(ref, width, blocks, degree_in_rows):
        odd = (2 * iota((16, width), 1) + 1).astype(F32)
        bs, bc = turn((2 * iota((16, width), 0) + 1).astype(F32) * odd, 4096.0)
        base = [with_phase(i, bs, bc) for i in range(2)]

        def rows(q, carry):
            first = q * 16
            sa, ca = turn((2 * first).astype(F32) * odd[:8], 4096.0)
            sa, ca = jnp.concatenate([sa, sa], axis=0), jnp.concatenate([ca, ca], axis=0)
            degree = first + iota((16, width), 0) if degree_in_rows else iota((16, width), 1)
            for i in range(2):
                sb, cb = base[i]
                value = jnp.where(degree.astype(F32) >= order_here[i], ca * cb - sa * sb, 0.0)
                ref[i, pl.ds(pl.multiple_of(first, 16), 16), :] = value.astype(BF)
            return carry

        lax.fori_loop(0, blocks, rows, 0)

    legendre_rows(leg, NLAT, LMAX // 16, True)
    legendre_rows(legt, LMAX, NLAT // 16, False)

    for dz in range(1, NZ):
        arrived = wg.at[(z + NZ - dz) % NZ, core]
        pltpu.make_async_copy(arrived, arrived, wrsem.at[dz]).wait()
    to_sibling = pltpu.make_async_remote_copy(
        src_ref=wg.at[:, core], dst_ref=wg.at[:, core], send_sem=wsem.at[1], recv_sem=wrsem.at[0],
        device_id=(sibling, z), device_id_type=MESH,
    )
    to_sibling.start()

    def project(phase, i):
        k = phase * 2 + i
        data = jnp.concatenate(
            [rcv[k, zz * NS : zz * NS + NS].reshape(NLAT, 128) for zz in range(NZ)], axis=1
        )
        return dot_nn(leg[i], data) * 0.0625

    def expand(phase, i):
        k = phase * 2 + i
        grid = dot_nn(legt[i], spec[i]) * 0.0625
        for zz in range(NZ):
            part = grid[:, zz * 128 : zz * 128 + 128].reshape(NS, LD, 128)
            snd[k, zz * NS : zz * NS + NS] = part.astype(BF)

    wait_all(0, 0)
    coeffs[0] = project(0, 0).astype(BF)

    to_sibling.wait_recv()
    for zz in range(NZ):
        for u in range(2):
            a = wg[zz, 0, u * CD : u * CD + CD].astype(F32)
            b = wg[zz, 1, u * CD : u * CD + CD].astype(F32)
            top = swap_halves(a, b)
            low = swap_halves(-b, a)
            for n in range(2):
                lanes = slice((2 * u + n) * 128, (2 * u + n) * 128 + 128)
                mat[zz * 128 : zz * 128 + CD, lanes] = top[n].astype(BF)
                mat[zz * 128 + CD : zz * 128 + 128, lanes] = low[n].astype(BF)
        fold = wg[zz, :, WROWS : WROWS + GROWS].astype(F32).reshape(320, 128)
        both = pltpu.roll(fold, 64, 1)
        low = low_half((320, 128))
        gains[0:320, zz * 128 : zz * 128 + 128] = jnp.where(low, fold, both).astype(BF)
        gains[320:640, zz * 128 : zz * 128 + 128] = jnp.where(low, both, fold).astype(BF)

    def mix(i):
        prod = dot_nn(coeffs[i], mat[...])
        mixed[i] = prod
        spec[i] = (gains[...].astype(F32) * prod).astype(BF)
        expand(1, i)
        start_all(1, i, False)

    mix(0)
    wait_all(0, 1)
    coeffs[1] = project(0, 1).astype(BF)
    mix(1)

    def order_rows(i, r):
        tiles = [scr[i, pl.ds(4 * g + r, ND, stride=LD), :] for g in range(4)]
        pairs = [swap_halves(tiles[0], tiles[1]), swap_halves(tiles[2], tiles[3])]
        parts = [jnp.concatenate([pairs[0][p], pairs[1][p]], axis=1) for p in range(2)]
        return jnp.concatenate(parts, axis=0).astype(BF)

    def unpack(phase, i):
        wait_all(phase, i)
        scr[i] = rcv[phase * 2 + i].astype(F32).reshape(ND * LD, 128)

    def grid_part(i, r):
        return dot_tn(order_rows(i, r), tab[r, i].reshape(ORD, WIN))

    def first_part(phase):
        unpack(phase, 0)
        for r in range(4):
            partial[r] = grid_part(0, r)

    def put_window(ref, r, value):
        for g in range(4):
            part = value[g * CD : g * CD + CD]
            lo = g * GROUP + STARTS[r]
            if r > 0:
                first = ref[:, lo : lo + 128].astype(F32) + part[:, :128]
                ref[:, lo : lo + 128] = first.astype(BF)
                ref[:, lo + 128 : lo + WIN] = part[:, 128:].astype(BF)
            else:
                ref[:, lo : lo + WIN] = part.astype(BF)

    cot_in.wait()
    first_part(1)
    unpack(1, 1)
    for r in range(4):
        before = (partial[r] + grid_part(1, r)) * 0.0625
        value, slope = gelu_parts(before)
        put_window(out_v, r, value)
        grads[r] = (window(cot_v, r).astype(F32) * slope).astype(BF)
        fourier_tiles(0, grads[r], r, 0.0625)
    pack_send(2, 0)
    start_all(2, 0, True)
    for r in range(4):
        fourier_tiles(1, grads[r], r, 0.0625)
    pack_send(2, 1)
    start_all(2, 1, True)

    def back(i):
        wait_all(2, i)
        value = project(2, i)
        here = value * mixed[i]
        gsum[...] = here if i == 0 else gsum[...] + here
        spec[i] = (gains[...].astype(F32) * value).astype(BF)
        if i == 0:
            wpart = dot_tn(coeffs[0], spec[0])
            mixed[0, :512] = wpart
        else:
            wpart = dot_tn(coeffs[1], spec[1]) + mixed[0, :512]
            sign = jnp.where(low_half((CD, 128)), 1.0, -1.0)
            for zz in range(NZ):
                for zo in range(NZ):
                    lanes = slice(zo * 128, zo * 128 + 128)
                    up = wpart[zz * 128 : zz * 128 + CD, lanes]
                    down = wpart[zz * 128 + CD : zz * 128 + 128, lanes]
                    redw[zz, zo * CD : zo * CD + CD] = (up + pltpu.roll(down, 64, 1) * sign).astype(BF)
                both = gsum[:, zz * 128 : zz * 128 + 128]
                both = both + pltpu.roll(both, 64, 1)
                redg[zz] = jnp.where(low_half((320, 128)), both[:320], both[320:]).astype(BF)

    def to_inputs(i):
        spec[i] = dot_nt(spec[i], mat[...]).astype(BF)

    back(0)
    to_inputs(0)
    expand(3, 0)
    start_all(3, 0, False)
    back(1)

    @pl.when(core == 0)
    def _():
        pltpu.make_async_remote_copy(
            src_ref=redg, dst_ref=pairg, send_sem=dsem.at[0], recv_sem=drsem.at[0],
            device_id=(sibling, z), device_id_type=MESH,
        ).start()

    @pl.when(core == 1)
    def _():
        pltpu.make_async_remote_copy(
            src_ref=redw, dst_ref=pairw, send_sem=dsem.at[0], recv_sem=drsem.at[0],
            device_id=(sibling, z), device_id_type=MESH,
        ).start()

    to_inputs(1)
    expand(3, 1)
    start_all(3, 1, False)

    source = xy * NZ + z

    @pl.when(core == 0)
    def _():
        pltpu.make_async_copy(pairw, pairw, drsem.at[0]).wait()
        pairw[...] = (pairw[...].astype(F32) + redw[...].astype(F32)).astype(BF)

        def go(n, carry):
            t = (source + n * 37) % (NXY * NZ)
            txy, tz = t // NZ, t % NZ
            pltpu.make_async_remote_copy(
                src_ref=pairw.at[tz, pl.ds(pl.multiple_of(txy * WCH, WCH), WCH)], dst_ref=inw.at[source],
                send_sem=dsem.at[1], recv_sem=drsem.at[1], device_id=(txy * 2, tz), device_id_type=MESH,
            ).start()
            return carry

        lax.fori_loop(1, NXY * NZ, go, 0)
        pltpu.make_async_copy(
            pairw.at[z, pl.ds(pl.multiple_of(xy * WCH, WCH), WCH)], inw.at[source], drsem.at[1]
        ).start()

    chunk = (xy * 5 + 7) // 8
    adds_gain = (chunk * 8) // 5 == xy

    @pl.when(core == 1)
    def _():
        pltpu.make_async_copy(pairg, pairg, drsem.at[0]).wait()
        pairg[...] = (pairg[...].astype(F32) + redg[...].astype(F32)).astype(BF)

        def go(n, carry):
            ch, tz = n % NG, (z + n // NG) % NZ
            txy = (ch * 8) // 5

            @pl.when(txy * NZ + tz != source)
            def _():
                pltpu.make_async_remote_copy(
                    src_ref=pairg.at[tz, pl.ds(pl.multiple_of(ch * GCH, GCH), GCH)], dst_ref=ing.at[source],
                    send_sem=dsem.at[2], recv_sem=drsem.at[2], device_id=(txy * 2 + 1, tz), device_id_type=MESH,
                ).start()

            @pl.when(txy * NZ + tz == source)
            def _():
                pltpu.make_async_copy(
                    pairg.at[tz, pl.ds(pl.multiple_of(ch * GCH, GCH), GCH)], ing.at[source], drsem.at[2]
                ).start()

            return carry

        lax.fori_loop(0, NG * NZ, go, 0)

    def share(mine, fin, at, sem):
        def go(n, carry):
            pltpu.make_async_remote_copy(
                src_ref=mine, dst_ref=fin.at[at], send_sem=dsem.at[sem], recv_sem=drsem.at[sem],
                device_id=((s + n) % NS, z), device_id_type=MESH,
            ).start()
            return carry

        lax.fori_loop(1, NS, go, 0)
        pltpu.make_async_copy(mine, fin.at[at], drsem.at[sem]).start()

    first_part(3)

    @pl.when(core == 0)
    def _():
        pltpu.make_async_copy(inw, inw, drsem.at[1]).wait()
        minew[...] = jnp.sum(inw[...].astype(F32), axis=0).astype(BF)
        share(minew, finw, xy, 3)

    @pl.when(jnp.logical_and(core == 1, adds_gain))
    def _():
        pltpu.make_async_copy(ing, ing, drsem.at[2]).wait()
        mineg[...] = jnp.sum(ing[...].astype(F32), axis=0).astype(BF)
        share(mineg, fing, chunk, 4)

    unpack(3, 1)
    for r in range(4):
        put_window(x_v, r, (partial[r] + grid_part(1, r)) * (1.0 / math.sqrt(NLON)))

    pltpu.make_async_copy(finw, finw, drsem.at[3]).wait()
    pltpu.make_async_copy(fing, fing, drsem.at[4]).wait()
    wscale = 1.0 / math.sqrt(ORD * LMAX)
    sums = finw[...].astype(F32).reshape(NZ, CD, 128) * wscale
    for u in range(2):
        pair = swap_halves(sums[2 * u], sums[2 * u + 1])
        for p in range(2):
            wgrad_ref[p, :, u * 128 : u * 128 + 128] = pair[p]
    fold = fing[...].astype(F32).reshape(320, 128) * (1.0 / math.sqrt(ORD))
    ggrad_ref[...] = jnp.transpose(jnp.concatenate([fold, pltpu.roll(fold, 64, 1)], axis=0))[:CD]

    for k in range(8):
        pltpu.make_async_copy(snd.at[k, pl.ds(0, ND - 1)], snd.at[k, pl.ds(0, ND - 1)], ssem.at[k]).wait()
    for dz in range(1, NZ):
        pltpu.make_async_copy(wg.at[z, core], wg.at[z, core], wsem.at[0]).wait()
    to_sibling.wait_send()

    @pl.when(core == 0)
    def _():
        pltpu.make_async_copy(redg, redg, dsem.at[0]).wait()
        others = NXY * NZ - 1
        pltpu.make_async_copy(inw.at[pl.ds(0, others)], inw.at[pl.ds(0, others)], dsem.at[1]).wait()
        pltpu.make_async_copy(sent(finw), sent(finw), dsem.at[3]).wait()
        pltpu.make_async_copy(rest(finw), rest(finw), dsem.at[3]).wait()

    @pl.when(core == 1)
    def _():
        pltpu.make_async_copy(redw, redw, dsem.at[0]).wait()

        @pl.when(adds_gain)
        def _():
            others = NG * NZ - 1
            pltpu.make_async_copy(ing.at[pl.ds(0, others)], ing.at[pl.ds(0, others)], dsem.at[2]).wait()
            for _ in range(3):
                pltpu.make_async_copy(fing, fing, dsem.at[4]).wait()
            pltpu.make_async_copy(mineg, mineg, dsem.at[4]).wait()

        @pl.when(jnp.logical_not(adds_gain))
        def _():
            others = NG * NZ
            pltpu.make_async_copy(ing.at[pl.ds(0, others)], ing.at[pl.ds(0, others)], dsem.at[2]).wait()


def sent(fin):
    return fin.at[pl.ds(0, NXY)]


def rest(fin):
    return fin.at[pl.ds(0, NXY - 1)]


def finish(*refs):
    sem = refs[-1]
    copies = [pltpu.make_async_copy(refs[i], refs[4 + i], sem.at[i]) for i in range(2, 4)]
    for n in range(4):
        rows = pl.ds(n * 16, 16)
        for i in range(2):
            copies.append(
                pltpu.make_async_copy(refs[i].at[rows], refs[4 + i].at[rows], sem.at[4 + 2 * n + i])
            )
    for copy in copies:
        copy.start()
    for copy in copies:
        copy.wait()


def body(fields, mixing_weight, degree_gain, cotangent, order_ids):
    cells = fields.shape[2]
    vmem = pl.BlockSpec(memory_space=pltpu.VMEM)
    anyw = pl.BlockSpec(memory_space=pl.ANY)
    smem = pl.BlockSpec(memory_space=pltpu.SMEM)
    shapes = (
        ((CD, cells), BF),
        ((CD, cells), BF),
        ((2, CD, 256), F32),
        ((CD, LMAX), F32),
    )
    results = pl.pallas_call(
        kernel,
        out_shape=tuple(pltpu.VMEM(shape, kind) for shape, kind in shapes),
        in_specs=[anyw, vmem, vmem, anyw, vmem, smem],
        out_specs=(vmem,) * 4,
        scratch_shapes=[
            pltpu.VMEM((CD, cells), BF),
            pltpu.VMEM((4, 2, 2, ND, WIN), BF),
            pltpu.VMEM((2, ND, 384), F32),
            pltpu.VMEM((2, LMAX, NLAT), BF),
            pltpu.VMEM((2, NLAT, LMAX), BF),
            pltpu.VMEM((2, ND * LD, 128), F32),
            pltpu.VMEM((4, 256, WIN), F32),
            pltpu.VMEM((4, 256, WIN), BF),
            pltpu.VMEM((8, ND, LD, 128), BF),
            pltpu.VMEM((8, ND, LD, 128), BF),
            pltpu.VMEM((2, GROWS, 128), BF),
            pltpu.VMEM((NZ, 2, WROWS + GROWS, 128), BF),
            pltpu.VMEM((512, 512), BF),
            pltpu.VMEM((LMAX, 512), BF),
            pltpu.VMEM((LMAX, 512), F32),
            pltpu.VMEM((2, LMAX, 512), F32),
            pltpu.VMEM((2, LMAX, 512), BF),
            pltpu.VMEM((2, LMAX, 512), BF),
            pltpu.VMEM((NZ, 256, 128), BF),
            pltpu.VMEM((NZ, 320, 128), BF),
            pltpu.VMEM((NZ, 256, 128), BF),
            pltpu.VMEM((NZ, 320, 128), BF),
            pltpu.VMEM((NXY * NZ, WCH, 128), BF),
            pltpu.VMEM((NXY * NZ, GCH, 128), BF),
            pltpu.VMEM((WCH, 128), BF),
            pltpu.VMEM((GCH, 128), BF),
            pltpu.VMEM((NXY, WCH, 128), BF),
            pltpu.VMEM((NG, GCH, 128), BF),
            pltpu.SemaphoreType.DMA((2,)),
            pltpu.SemaphoreType.DMA((8,)),
            pltpu.SemaphoreType.DMA((8,)),
            pltpu.SemaphoreType.DMA((2,)),
            pltpu.SemaphoreType.DMA((4,)),
            pltpu.SemaphoreType.DMA((5,)),
            pltpu.SemaphoreType.DMA((5,)),
        ],
        compiler_params=pltpu.CompilerParams(
            collective_id=0, has_side_effects=True, vmem_limit_bytes=50 << 20
        ),
    )(
        fields.reshape(CD, cells), mixing_weight, degree_gain.T, cotangent.reshape(CD, cells),
        order_ids.reshape(1, ORD), order_ids,
    )
    out, fgrad, wgrad, ggrad = pl.pallas_call(
        finish,
        out_shape=tuple(jax.ShapeDtypeStruct(shape, kind) for shape, kind in shapes),
        in_specs=[anyw] * 4,
        out_specs=(anyw,) * 4,
        scratch_shapes=[pltpu.SemaphoreType.DMA((12,))],
        compiler_params=pltpu.CompilerParams(vmem_limit_bytes=1 << 20),
    )(*[pltpu.with_memory_space_constraint(a, pltpu.VMEM) for a in results])
    return out.reshape(1, CD, cells), fgrad.reshape(1, CD, cells), wgrad, ggrad.T


def solution(mesh):
    return jax.shard_map(
        body,
        mesh=mesh,
        in_specs=(
            P(None, "chan", "spatial"),
            P(None, "chan", None),
            P(None, "chan"),
            P(None, "chan", "spatial"),
            P(),
        ),
        out_specs=(
            P(None, "chan", "spatial"),
            P(None, "chan", "spatial"),
            P(None, "chan", None),
            P(None, "chan"),
        ),
        check_vma=False,
    )
```
